512 devices in a mesh: row: 32 (over y, x, core), col: 16 (over z).
Axes of the slice: x: 4, y: 4, z: 16, core: 2. Of those that a mesh axis runs over, the one named last changes fastest.
Arguments:
- blocks: float32 [16, 96, 4, 256, 256], P('col', 'row'), may hold values from -0.046875 to 0.046875
- block_cols: int32 [16, 96, 4], P('col', 'row'), may hold values from 0 to 191, as said below
- block_slot: int32 [16, 192], P('col'), may hold values from 0 to 191, as said below
- trials: float32 [16, 192, 32, 256], P('col', 'row'), may hold values from -6 to 6
- basis: float32 [32, 24576], P(None, ('row', 'col'))
- ritz_terms: float32 [32, 32], replicated, may hold values from -332.55374 to 332.55374
Outputs:
- sigma: float32 [32, 24576], P(None, ('row', 'col'))
- corrections: float32 [32, 24576], P(None, ('row', 'col'))
The draws below stay inside these ranges and needn't reach their ends.
Inputs may be any that keep to these rules, and one draw needn't show every extreme that they name: `block_slot`: each row of one column group is a permutation of the storage slots 0 to 191. `block_cols`: the 12 block columns of one device (its 3 block rows) are all different; among them at most 1 have storage slots on one index of row (slot // 6 equal), and some index has exactly 1.
All inputs are finite; a program needn't handle non-finite values.
Results may differ from the reference program's by a relative error of at most 0.00014.
Values sent between devices are 32-bit elements; how exact they have to be, the bound alone decides.
No kernel may reach another device: no remote copies, remote signals or barrier semaphores. Data moves between devices by JAX's collectives and lax.ppermute only.
A program may use at most 64 MiB of HBM per device.

```python
import jax
import jax.numpy as jnp
from jax import lax

BS = 256
K = 32
NB = 32
BR_DEV = 3
NZ_ROW = 4
VB_DEV = 6
CBLK = 192
SLAB = 24576
N_ROW = 32
N_COL = 16


def slot_table(key):
    keys = jax.random.split(key, N_COL)
    return jax.vmap(lambda single: jax.random.permutation(single, CBLK))(keys).astype(jnp.int32)


def draw_block_slot(key, part):
    return slot_table(key)


def draw_block_cols(key, part):
    table = slot_table(key)
    key = jax.random.fold_in(key, 7)
    count = BR_DEV * NZ_ROW
    most = (count + N_ROW - 1) // N_ROW
    group_ids = jnp.arange(N_COL, dtype=jnp.int32)
    row_ids = jnp.arange(N_ROW, dtype=jnp.int32)

    def one_device(index, row_table):
        single = jax.random.fold_in(key, index)
        first_key = jax.random.fold_in(single, 1)
        second_key = jax.random.fold_in(single, 2)
        picks = jax.random.permutation(first_key, N_ROW * most)[:count].astype(jnp.int32)
        owner = picks // most
        place = picks % most
        offsets = jax.random.randint(second_key, (N_ROW,), 0, VB_DEV).astype(jnp.int32)
        inner = (offsets[owner] + place) % VB_DEV
        slots = owner * VB_DEV + inner
        inverse = jnp.argsort(row_table, stable=True).astype(jnp.int32)
        return inverse[slots].reshape(BR_DEV, NZ_ROW)

    def one_group(group, row_table):
        return jax.vmap(lambda row: one_device(group * N_ROW + row, row_table))(row_ids)
    result = jax.vmap(one_group)(group_ids, table)
    return result.reshape(N_COL, N_ROW * BR_DEV, NZ_ROW).astype(jnp.int32)


def draw_basis(key, part):
    key = jax.random.fold_in(key, 11)
    values = jax.random.normal(key, (NB, SLAB), jnp.float32)
    ramp = 1.0 + 2.0 * jnp.arange(SLAB, dtype=jnp.float32) / SLAB
    return (values * ramp[None, :] * (0.5 / SLAB ** 0.5)).astype(jnp.float32)


def steps_of(rng, shape, cuts, smallest, top_value):
    loudness = 1.0
    for dim, blocks in cuts:
        draws = jax.random.uniform(jax.random.fold_in(jax.random.fold_in(rng, 6), dim), (blocks,), jnp.float32, smallest / len(cuts), top_value / len(cuts))
        loudness = loudness * jnp.repeat(jnp.exp(draws), shape[dim] // blocks).reshape((-1,) + (1,) * (len(shape) - 1 - dim))
    return loudness


def scatter_about(key, shape, deviation, limit, pieces=(), held_as=jnp.bfloat16):
    loudness = steps_of(key, shape, pieces, -0.22, 0.18) if pieces else 1.0
    drawn = jax.random.normal(key, shape, jnp.float32) * deviation * loudness
    return jnp.minimum(jnp.maximum(drawn, -limit), limit).astype(held_as)


def setup_inputs(seed: int = 0) -> dict:
    key_of = jax.random.split(jax.random.key(seed), 7)
    blocks = scatter_about(key_of[0], (N_COL, BR_DEV * N_ROW, NZ_ROW, BS, BS), (NZ_ROW * N_COL * BS) ** -0.5, 0.046875, ((0, 16), (1, 32)), jnp.float32)
    block_cols = draw_block_cols(jax.random.fold_in(key_of[6], 71), 0)
    block_slot = draw_block_slot(jax.random.fold_in(key_of[6], 71), 0)
    trials = scatter_about(key_of[3], (N_COL, CBLK, K, BS), 1.0, 6.0, ((0, 16), (1, 32)), jnp.float32)
    basis = draw_basis(jax.random.fold_in(key_of[6], 71), 0)
    ritz_terms = scatter_about(key_of[5], (NB, K), ((4 * SLAB // NB) ** 0.5), 332.55374, (), jnp.float32)
    return dict(blocks=blocks, block_cols=block_cols, block_slot=block_slot, trials=trials, basis=basis, ritz_terms=ritz_terms)


def group_term(carry, inputs):
    group_blocks, group_cols, group_slot, group_trials = inputs
    slots = group_slot[group_cols]
    chosen = group_trials[slots]
    term = jnp.einsum("rnij,rnkj->kri", group_blocks, chosen, precision=lax.Precision.HIGHEST)
    return carry + term, None


def reference(blocks, block_cols, block_slot, trials, basis, ritz_terms):
    rows = blocks.shape[1]
    start = jnp.zeros((K, rows, BS), jnp.float32)
    total, unused = lax.scan(group_term, start, (blocks, block_cols, block_slot, trials))
    sigma = total.reshape(K, rows * BS)
    high = lax.Precision.HIGHEST
    resid = sigma - jnp.dot(ritz_terms.T, basis, precision=high)
    first = jnp.dot(basis, resid.T, precision=high)
    projected = resid - jnp.dot(first.T, basis, precision=high)
    second = jnp.dot(basis, projected.T, precision=high)
    corrections = projected - jnp.dot(second.T, basis, precision=high)
    return sigma, corrections
```

```python
import functools

import jax
import jax.numpy as jnp
from jax import lax
from jax.experimental import pallas as pl
from jax.experimental.pallas import tpu as pltpu
from jax.sharding import PartitionSpec as P

LANES = 128
HIGH = lax.Precision.HIGHEST
SMEM = pl.BlockSpec(memory_space=pltpu.SMEM)
VMEM = pl.BlockSpec(memory_space=pltpu.VMEM)
NT = (((1,), (1,)), ((), ()))
TN = (((0,), (0,)), ((), ()))


def slot_of(cols_ref, table_ref, entry):
    return table_ref[cols_ref[entry]]


def request_kernel(stored, cols_ref, table_ref, out_ref):
    owners = lax.broadcasted_iota(jnp.int32, out_ref.shape, 0)
    wanted = jnp.zeros(out_ref.shape, jnp.int32)
    for entry in range(cols_ref.shape[0]):
        slot = slot_of(cols_ref, table_ref, entry)
        owner = slot // stored
        wanted = jnp.where(owners == owner, slot - owner * stored, wanted)
    out_ref[...] = wanted


def pick_kernel(wanted_ref, trials_ref, out_ref):
    for dest in range(out_ref.shape[0]):
        out_ref[dest] = trials_ref[wanted_ref[dest, 0]]


def split(value):
    top = value.astype(jnp.bfloat16)
    rest = (value - top.astype(jnp.float32)).astype(jnp.bfloat16)
    return top, rest


def partial_kernel(
    stored, cols_ref, table_ref, blocks_ref, chosen_ref, basis_ref, out_ref, gram_ref, part, wide, bwide
):
    rows, per_row, size, _ = blocks_ref.shape
    vectors = chosen_ref.shape[1]
    groups, _, width = basis_ref.shape
    for row in range(rows):
        total = jnp.zeros((vectors, size), jnp.float32)
        for entry in range(per_row):
            owner = slot_of(cols_ref, table_ref, row * per_row + entry) // stored
            vec_top, vec_rest = split(chosen_ref[owner])
            mat_top, mat_rest = split(blocks_ref[row, entry])
            both = jnp.concatenate([vec_top, vec_rest], axis=0)
            first = lax.dot_general(both, mat_top, NT, preferred_element_type=jnp.float32)
            second = lax.dot_general(vec_top, mat_rest, NT, preferred_element_type=jnp.float32)
            total += first[:vectors] + (first[vectors:] + second)
        part[:, row * size : (row + 1) * size] = total
    chunk = rows * size // groups
    pad = jnp.zeros((vectors, LANES - chunk), jnp.float32)
    for group in range(groups):
        wide[:, group * LANES : (group + 1) * LANES] = jnp.concatenate(
            [part[:, group * chunk : (group + 1) * chunk], pad], axis=1
        )
        bwide[:, group * LANES : (group + 1) * LANES] = jnp.concatenate([basis_ref[group], pad], axis=1)
    moments = lax.dot_general(bwide[...], wide[...], NT, precision=HIGH, preferred_element_type=jnp.float32)
    gram_ref[...] = lax.dot_general(
        bwide[...], bwide[...], NT, precision=HIGH, preferred_element_type=jnp.float32
    )
    for group in range(groups):
        out_ref[group] = wide[:, group * LANES : (group + 1) * LANES]
        out_ref[group, :, chunk : chunk + vectors] = moments


def sum_kernel(recv_ref, gram_ref, sigma_ref, out_ref):
    groups = recv_ref.shape[0]
    chunk = sigma_ref.shape[1]
    nb = gram_ref.shape[0]
    total = recv_ref[0]
    for group in range(1, groups):
        total = total + recv_ref[group]
    sigma_ref[...] = total[:, :chunk]
    moments = total[:, chunk : chunk + nb]
    gram = gram_ref[...]
    half = nb // 2
    packed = jnp.concatenate([moments[:half], moments[half:], gram[:half], gram[half:]], axis=1)
    for dest in range(out_ref.shape[0]):
        out_ref[dest] = packed


def final_kernel(recv_ref, sigma_ref, basis_ref, ritz_ref, out_ref):
    total = recv_ref[0]
    for source in range(1, recv_ref.shape[0]):
        total = total + recv_ref[source]
    nb = ritz_ref.shape[0]
    moments = jnp.concatenate([total[:, :nb], total[:, nb : 2 * nb]], axis=0)
    gram = jnp.concatenate([total[:, 2 * nb : 3 * nb], total[:, 3 * nb :]], axis=0)
    ritz = ritz_ref[...]
    dot = functools.partial(jnp.dot, precision=HIGH, preferred_element_type=jnp.float32)
    first = moments - dot(gram, ritz)
    second = first - dot(gram, first)
    weights = ritz + first + second
    out_ref[...] = sigma_ref[...] - lax.dot_general(
        weights, basis_ref[...], TN, precision=HIGH, preferred_element_type=jnp.float32
    )


def shape(*dims, dtype=jnp.float32):
    return jax.ShapeDtypeStruct(dims, dtype)


def per_device(n_row, n_col, blocks, block_cols, block_slot, trials, basis, ritz_terms):
    local = blocks[0]
    rows, per_row, size, _ = local.shape
    owned = trials[0]
    stored, vectors, _ = owned.shape
    nb, chunk = basis.shape
    cols = block_cols.reshape(rows * per_row)
    table = block_slot.reshape(block_slot.shape[1])
    params = pltpu.CompilerParams(vmem_limit_bytes=32 * 1024 * 1024)

    requests = pl.pallas_call(
        functools.partial(request_kernel, stored),
        out_shape=shape(n_row, LANES, dtype=jnp.int32),
        in_specs=[SMEM, SMEM],
        out_specs=VMEM,
        compiler_params=params,
    )(cols, table)
    wanted = lax.all_to_all(requests, "row", 0, 0, tiled=True)
    sent = pl.pallas_call(
        pick_kernel,
        out_shape=shape(n_row, vectors, size),
        in_specs=[SMEM, VMEM],
        out_specs=VMEM,
        compiler_params=params,
    )(wanted, owned)
    chosen = lax.all_to_all(sent, "row", 0, 0, tiled=True)
    spread = jnp.broadcast_to(basis[None], (n_col, nb, chunk))
    row_basis = lax.all_to_all(spread, "col", 0, 0, tiled=True)

    partial_sums, gram = pl.pallas_call(
        functools.partial(partial_kernel, stored),
        out_shape=(shape(n_col, vectors, LANES), shape(nb, nb)),
        in_specs=[SMEM, SMEM, VMEM, VMEM, VMEM],
        out_specs=(VMEM, VMEM),
        scratch_shapes=[
            pltpu.VMEM((vectors, rows * size), jnp.float32),
            pltpu.VMEM((vectors, n_col * LANES), jnp.float32),
            pltpu.VMEM((nb, n_col * LANES), jnp.float32),
        ],
        compiler_params=params,
    )(cols, table, local, chosen, row_basis)
    gathered = lax.all_to_all(partial_sums, "col", 0, 0, tiled=True)
    sigma, moments = pl.pallas_call(
        sum_kernel,
        out_shape=(shape(vectors, chunk), shape(n_row, nb // 2, LANES)),
        in_specs=[VMEM, VMEM],
        out_specs=(VMEM, VMEM),
        compiler_params=params,
    )(gathered, gram)
    all_moments = lax.all_to_all(moments, "row", 0, 0, tiled=True)
    corrections = pl.pallas_call(
        final_kernel,
        out_shape=shape(vectors, chunk),
        in_specs=[VMEM, VMEM, VMEM, VMEM],
        out_specs=VMEM,
        compiler_params=params,
    )(all_moments, sigma, basis, ritz_terms)
    return sigma, corrections


def solution(mesh):
    in_specs = (
        P("col", "row", None, None, None),
        P("col", "row", None),
        P("col", None),
        P("col", "row", None, None),
        P(None, ("row", "col")),
        P(),
    )
    out_specs = (P(None, ("row", "col")), P(None, ("row", "col")))
    body = functools.partial(per_device, mesh.shape["row"], mesh.shape["col"])
    return jax.shard_map(body, mesh=mesh, in_specs=in_specs, out_specs=out_specs, check_vma=False)
```

```python
import functools

import jax
import jax.numpy as jnp
from jax import lax
from jax.experimental import pallas as pl
from jax.experimental.pallas import tpu as pltpu
from jax.sharding import PartitionSpec as P

LANES = 128
HIGH = lax.Precision.HIGHEST
SMEM = pl.BlockSpec(memory_space=pltpu.SMEM)
VMEM = pl.BlockSpec(memory_space=pltpu.VMEM)
HBM = pl.BlockSpec(memory_space=pltpu.HBM)
NT = (((1,), (1,)), ((), ()))
TN = (((0,), (0,)), ((), ()))
STEPS = (1, 8, 4, 2)
REQUEST_ROWS = 2
EARLY = 2


def slot_of(cols_ref, table_ref, row, entry):
    return table_ref[0, cols_ref[row, 0, entry]]


def request_kernel(
    cols_hbm, table_hbm, basis_hbm, trials_hbm, out_ref, packed_ref, trials_ref, cols, table, basis_ref, sems
):
    copies = [
        pltpu.make_async_copy(source, target, sems.at[index])
        for index, (source, target) in enumerate(
            [(cols_hbm, cols), (table_hbm, table), (basis_hbm, basis_ref), (trials_hbm, trials_ref)]
        )
    ]
    for copy in copies:
        copy.start()
    stored = trials_ref.shape[0]
    copies[0].wait()
    copies[1].wait()
    owners = lax.broadcasted_iota(jnp.int32, out_ref.shape, 0) // REQUEST_ROWS
    wanted = jnp.zeros(out_ref.shape, jnp.int32)
    for row in range(cols.shape[0]):
        for entry in range(cols.shape[2]):
            slot = slot_of(cols, table, row, entry)
            owner = slot // stored
            wanted = jnp.where(owners == owner, slot - owner * stored, wanted)
    out_ref[...] = wanted
    copies[2].wait()
    basis = basis_ref[...]
    half, chunk = basis.shape[0] // 2, basis.shape[1]
    pad = jnp.zeros((half, LANES - 2 * chunk), jnp.float32)
    packed_ref[0] = jnp.concatenate([basis[:half], basis[half:], pad], axis=1)
    copies[3].wait()


def join_kernel(left_ref, right_ref, out_ref):
    count = left_ref.shape[0]
    out_ref[:count] = left_ref[...]
    out_ref[count:] = right_ref[...]


def pick_kernel(wanted_ref, trials_ref, out_ref):
    dests, vectors, size = out_ref.shape
    stored = trials_ref.shape[0]
    for dest in range(dests):
        want = jnp.broadcast_to(wanted_ref[dest * REQUEST_ROWS : dest * REQUEST_ROWS + 1, :], (8, LANES))
        masks = [want == index for index in range(1, stored)]
        for top in range(0, vectors, 8):
            for left in range(0, size, LANES):
                tile = trials_ref[0, top : top + 8, left : left + LANES]
                for index in range(1, stored):
                    other = trials_ref[index, top : top + 8, left : left + LANES]
                    tile = jnp.where(masks[index - 1], other, tile)
                out_ref[dest, top : top + 8, left : left + LANES] = tile


def split(value):
    top = value.astype(jnp.bfloat16)
    rest = (value - top.astype(jnp.float32)).astype(jnp.bfloat16)
    return top, rest


def load_kernel(blocks_hbm, out_ref, sem):
    copy = pltpu.make_async_copy(blocks_hbm.at[: out_ref.shape[0]], out_ref, sem)
    copy.start()
    copy.wait()


def place_of(relative):
    place = 0
    for order, step in enumerate(STEPS):
        place = place + ((relative // step) % 2) * (1 << order)
    return place


def basis_kernel(packed_ref, out_ref):
    groups, half, _ = packed_ref.shape
    chunk = out_ref.shape[1] // groups
    own = lax.axis_index("col")
    for group in range(groups):
        both = packed_ref[place_of(jnp.bitwise_xor(own, group))]
        here = slice(group * chunk, (group + 1) * chunk)
        out_ref[:, here] = jnp.concatenate([both[:, :chunk], both[:, chunk : 2 * chunk]], axis=0)


def gram_kernel(basis_ref, out_ref):
    basis = basis_ref[...]
    out_ref[...] = lax.dot_general(basis, basis, NT, precision=HIGH, preferred_element_type=jnp.float32)


def partial_kernel(
    stored, cols_ref, table_ref, held_ref, blocks_hbm, chosen_ref, basis_ref, out_ref, part, late, sems
):
    rows, per_row, size, _ = blocks_hbm.shape
    held = held_ref.shape[0]
    vectors = chosen_ref.shape[1]
    groups = out_ref.shape[0]
    copies = [
        pltpu.make_async_copy(blocks_hbm.at[row], late.at[row - held], sems.at[row - held])
        for row in range(held, rows)
    ]
    for copy in copies:
        copy.start()
    for row in range(rows):
        if row >= held:
            copies[row - held].wait()
        total = jnp.zeros((vectors, size), jnp.float32)
        for entry in range(per_row):
            owner = slot_of(cols_ref, table_ref, row, entry) // stored
            vec_top, vec_rest = split(chosen_ref[owner])
            block = held_ref[row, entry] if row < held else late[row - held, entry]
            mat_top, mat_rest = split(block)
            both = jnp.concatenate([vec_top, vec_rest], axis=0)
            first = lax.dot_general(both, mat_top, NT, preferred_element_type=jnp.float32)
            second = lax.dot_general(vec_top, mat_rest, NT, preferred_element_type=jnp.float32)
            total += first[:vectors] + (first[vectors:] + second)
        part[:, row * size : (row + 1) * size] = total
    moments = lax.dot_general(
        basis_ref[...], part[...], NT, precision=HIGH, preferred_element_type=jnp.float32
    )
    half, quarter = vectors // 2, vectors // 4
    chunk = rows * size // groups
    pad = jnp.zeros((quarter, LANES - 2 * vectors), jnp.float32)
    low = jnp.concatenate([moments[half : half + quarter], moments[half + quarter :], pad], axis=1)
    for group in range(groups):
        here = slice(group * chunk, (group + 1) * chunk)
        out_ref[group, :half] = jnp.concatenate([part[:half, here], part[half:, here], moments[:half]], axis=1)
        out_ref[group, half:] = low


def sum_kernel(recv_ref, gram_ref, sigma_ref, keep_ref, out_ref):
    vectors, chunk = sigma_ref.shape
    half, quarter = vectors // 2, vectors // 4
    total = recv_ref[0]
    for group in range(1, recv_ref.shape[0]):
        total = total + recv_ref[group]
    sigma = jnp.concatenate([total[:half, :chunk], total[:half, chunk : 2 * chunk]], axis=0)
    sigma_ref[...] = sigma
    keep_ref[...] = sigma
    low = jnp.concatenate([total[half:, :vectors], total[half:, vectors : 2 * vectors]], axis=0)
    gram = gram_ref[...]
    packed = jnp.concatenate([total[:half, 2 * chunk :], low, gram[:half], gram[half:]], axis=1)
    for dest in range(out_ref.shape[0]):
        out_ref[dest] = packed


def final_kernel(recv_ref, sigma_ref, basis_ref, ritz_ref, out_ref):
    total = recv_ref[0]
    for source in range(1, recv_ref.shape[0]):
        total = total + recv_ref[source]
    nb = ritz_ref.shape[0]
    moments = jnp.concatenate([total[:, :nb], total[:, nb : 2 * nb]], axis=0)
    gram = jnp.concatenate([total[:, 2 * nb : 3 * nb], total[:, 3 * nb :]], axis=0)
    ritz = ritz_ref[...]
    dot = functools.partial(jnp.dot, precision=HIGH, preferred_element_type=jnp.float32)
    first = moments - dot(gram, ritz)
    second = first - dot(gram, first)
    weights = ritz + first + second
    out_ref[...] = sigma_ref[...] - lax.dot_general(
        weights, basis_ref[...], TN, precision=HIGH, preferred_element_type=jnp.float32
    )


def shape(*dims, dtype=jnp.float32):
    return jax.ShapeDtypeStruct(dims, dtype)


def call(kernel, outs, ins, operands, scratch=()):
    single = not isinstance(outs, tuple)
    return pl.pallas_call(
        kernel,
        out_shape=outs,
        in_specs=ins,
        out_specs=VMEM if single else (VMEM,) * len(outs),
        scratch_shapes=list(scratch),
        compiler_params=pltpu.CompilerParams(vmem_limit_bytes=16 * 1024 * 1024),
    )(*operands)


def per_device(n_row, n_col, blocks, block_cols, block_slot, trials, basis, ritz_terms):
    local = blocks[0]
    rows, per_row, size, _ = local.shape
    stored, vectors, _ = trials.shape[1:]
    nb, chunk = basis.shape
    cols = jnp.transpose(block_cols, (1, 0, 2))
    local, owned, cols_hbm, table_hbm, basis_hbm = (
        pltpu.with_memory_space_constraint(value, pltpu.HBM)
        for value in (local, trials[0], cols, block_slot, basis)
    )
    half = nb // 2

    requests, packed, owned = call(
        request_kernel,
        (
            shape(n_row * REQUEST_ROWS, LANES, dtype=jnp.int32),
            shape(1, half, LANES),
            shape(stored, vectors, size),
        ),
        [HBM, HBM, HBM, HBM],
        (cols_hbm, table_hbm, basis_hbm, owned),
        [
            pltpu.SMEM(cols.shape, jnp.int32),
            pltpu.SMEM(block_slot.shape, jnp.int32),
            pltpu.VMEM(basis.shape, jnp.float32),
            pltpu.SemaphoreType.DMA((4,)),
        ],
    )
    wanted = lax.all_to_all(requests, "row", 0, 0, tiled=True)

    def neighbour(value, step):
        return lax.ppermute(value, "col", [(i, i ^ step) for i in range(n_col)])

    def join(left, right):
        return call(join_kernel, shape(2 * left.shape[0], half, LANES), [VMEM, VMEM], (left, right))

    for step in STEPS[:EARLY]:
        other = neighbour(packed, step)
        if step == STEPS[EARLY - 1]:
            break
        packed = join(packed, other)
    sent = call(pick_kernel, shape(n_row, vectors, size), [VMEM, VMEM], (wanted, owned))
    sent, other = lax.optimization_barrier((sent, other))
    chosen = lax.all_to_all(sent, "row", 0, 0, tiled=True)
    packed = join(packed, other)
    for step in STEPS[EARLY:]:
        packed = join(packed, neighbour(packed, step))
    held = 1
    early = call(
        load_kernel, shape(held, per_row, size, size), [HBM], (local,), [pltpu.SemaphoreType.DMA]
    )
    row_basis = call(basis_kernel, shape(nb, n_col * chunk), [VMEM], (packed,))
    gram = call(gram_kernel, shape(nb, nb), [VMEM], (row_basis,))

    partial_sums = call(
        functools.partial(partial_kernel, stored),
        shape(n_col, half + half // 2, LANES),
        [SMEM, SMEM, VMEM, HBM, VMEM, VMEM],
        (cols, block_slot, early, local, chosen, row_basis),
        [
            pltpu.VMEM((vectors, rows * size), jnp.float32),
            pltpu.VMEM((rows - held, per_row, size, size), jnp.float32),
            pltpu.SemaphoreType.DMA((rows - held,)),
        ],
    )
    gathered = lax.all_to_all(partial_sums, "col", 0, 0, tiled=True)
    sigma, keep, moments = call(
        sum_kernel,
        (shape(vectors, chunk), shape(vectors, chunk), shape(n_row, half, LANES)),
        [VMEM, VMEM],
        (gathered, gram),
    )
    all_moments = lax.all_to_all(moments, "row", 0, 0, tiled=True)
    corrections = call(
        final_kernel,
        shape(vectors, chunk),
        [VMEM, VMEM, VMEM, VMEM],
        (all_moments, keep, basis, ritz_terms),
    )
    return sigma, corrections


def solution(mesh):
    in_specs = (
        P("col", "row", None, None, None),
        P("col", "row", None),
        P("col", None),
        P("col", "row", None, None),
        P(None, ("row", "col")),
        P(),
    )
    out_specs = (P(None, ("row", "col")), P(None, ("row", "col")))
    body = functools.partial(per_device, mesh.shape["row"], mesh.shape["col"])
    return jax.shard_map(body, mesh=mesh, in_specs=in_specs, out_specs=out_specs, check_vma=False)
```

```python
import functools

import jax
import jax.numpy as jnp
from jax import lax
from jax.experimental import pallas as pl
from jax.experimental.pallas import tpu as pltpu
from jax.sharding import PartitionSpec as P

LANES = 128
HIGH = lax.Precision.HIGHEST
SMEM = pl.BlockSpec(memory_space=pltpu.SMEM)
VMEM = pl.BlockSpec(memory_space=pltpu.VMEM)
HBM = pl.BlockSpec(memory_space=pltpu.HBM)
NT = (((1,), (1,)), ((), ()))
TN = (((0,), (0,)), ((), ()))
CORES = 2
PACKED = 12


def pack(value):
    quarters = [value[8 * i : 8 * i + 8] for i in range(4)]
    cut = LANES - 2 * value.shape[1]
    upper = jnp.concatenate([quarters[0], quarters[1], quarters[2][:, :cut]], axis=1)
    rest = jnp.concatenate([quarters[2][:, cut:], quarters[3]], axis=1)
    return jnp.concatenate([upper, jnp.concatenate([rest[:4], rest[4:]], axis=1)], axis=0)


def unpack(rows, chunk):
    cut = LANES - 2 * chunk
    upper = rows[:8]
    rest = jnp.concatenate([rows[8:, : LANES // 2], rows[8:, LANES // 2 :]], axis=0)
    third = jnp.concatenate([upper[:, 2 * chunk :], rest[:, : chunk - cut]], axis=1)
    return jnp.concatenate(
        [upper[:, :chunk], upper[:, chunk : 2 * chunk], third, rest[:, chunk - cut :]], axis=0
    )


def put_rows(out_ref, group, start, rows):
    for row in range(rows.shape[0]):
        here = slice((start + row) * LANES, (start + row + 1) * LANES)
        out_ref[group, :, here] = rows[row : row + 1]


def slot_of(cols_ref, table_ref, row, entry):
    return table_ref[0, cols_ref[row, 0, entry]]


def spread_kernel(basis_ref, out_ref):
    packed = pack(basis_ref[...])
    for dest in range(out_ref.shape[0]):
        put_rows(out_ref, dest, 0, packed)


def request_kernel(cols_hbm, table_hbm, out_ref, cols, table, sems, *, stored):
    copies = [
        pltpu.make_async_copy(source, target, sems.at[index])
        for index, (source, target) in enumerate([(cols_hbm, cols), (table_hbm, table)])
    ]
    for copy in copies:
        copy.start()
    for copy in copies:
        copy.wait()
    owners = lax.broadcasted_iota(jnp.int32, out_ref.shape, 0)
    wanted = jnp.zeros(out_ref.shape, jnp.int32)
    for row in range(cols.shape[0]):
        for entry in range(cols.shape[2]):
            slot = slot_of(cols, table, row, entry)
            owner = slot // stored
            wanted = jnp.where(owners == owner, slot - owner * stored, wanted)
    out_ref[...] = wanted


def pick_kernel(wanted_ref, own_hbm, other_hbm, out_ref, pair, sems):
    dests, vectors, size = out_ref.shape
    stored = own_hbm.shape[0]
    core = lax.axis_index("row") % CORES
    copies = [
        pltpu.make_async_copy(own_hbm, pair.at[core], sems.at[0]),
        pltpu.make_async_copy(other_hbm, pair.at[1 - core], sems.at[1]),
    ]
    for copy in copies:
        copy.start()
    for copy in copies:
        copy.wait()
    for dest in range(dests):
        owner = dest % CORES
        want = jnp.broadcast_to(wanted_ref[dest : dest + 1, :], (8, LANES))
        masks = [want == index for index in range(1, stored)]
        for top in range(0, vectors, 8):
            for left in range(0, size, LANES):
                here = (slice(top, top + 8), slice(left, left + LANES))
                tile = pair[owner, 0, *here]
                for index in range(1, stored):
                    tile = jnp.where(masks[index - 1], pair[owner, index, *here], tile)
                out_ref[dest, *here] = tile


def split(value):
    top = value.astype(jnp.bfloat16)
    rest = (value - top.astype(jnp.float32)).astype(jnp.bfloat16)
    return top, rest


def basis_kernel(packed_ref, out_ref, rows):
    groups = packed_ref.shape[0]
    chunk = out_ref.shape[1] // groups
    for group in range(groups):
        for row in range(PACKED):
            rows[row : row + 1] = packed_ref[group, :, row * LANES : (row + 1) * LANES]
        out_ref[:, group * chunk : (group + 1) * chunk] = unpack(rows[:PACKED], chunk)


def gram_kernel(basis_ref, out_ref):
    basis = basis_ref[...]
    out_ref[...] = lax.dot_general(basis, basis, NT, precision=HIGH, preferred_element_type=jnp.float32)


def partial_kernel(stored, cols_ref, table_ref, blocks_ref, chosen_ref, basis_ref, out_ref, part):
    rows, per_row, size, _ = blocks_ref.shape
    vectors = chosen_ref.shape[1]
    groups = out_ref.shape[0]
    for row in range(rows):
        total = jnp.zeros((vectors, size), jnp.float32)
        for entry in range(per_row):
            owner = slot_of(cols_ref, table_ref, row, entry) // stored
            vec_top, vec_rest = split(chosen_ref[owner])
            mat_top, mat_rest = split(blocks_ref[row, entry])
            both = jnp.concatenate([vec_top, vec_rest], axis=0)
            first = lax.dot_general(both, mat_top, NT, preferred_element_type=jnp.float32)
            second = lax.dot_general(vec_top, mat_rest, NT, preferred_element_type=jnp.float32)
            total += first[:vectors] + (first[vectors:] + second)
        part[:, row * size : (row + 1) * size] = total
    moments = lax.dot_general(
        basis_ref[...], part[...], NT, precision=HIGH, preferred_element_type=jnp.float32
    )
    quarter = vectors // 4
    chunk = rows * size // groups
    tail = jnp.concatenate([moments[i * quarter : (i + 1) * quarter] for i in range(4)], axis=1)
    for group in range(groups):
        put_rows(out_ref, group, 0, pack(part[:, group * chunk : (group + 1) * chunk]))
        put_rows(out_ref, group, PACKED, tail)


def sum_kernel(recv_ref, gram_ref, sigma_ref, keep_ref, out_ref, rows):
    vectors, chunk = sigma_ref.shape
    half, quarter = vectors // 2, vectors // 4
    for row in range(PACKED + quarter):
        here = slice(row * LANES, (row + 1) * LANES)
        total = recv_ref[0, :, here]
        for group in range(1, recv_ref.shape[0]):
            total = total + recv_ref[group, :, here]
        place = row if row < PACKED else row - PACKED + 16
        rows[place : place + 1] = total
    sigma = unpack(rows[:PACKED], chunk)
    sigma_ref[...] = sigma
    keep_ref[...] = sigma
    tail = rows[16 : 16 + quarter]
    moments = jnp.concatenate([tail[:, i * vectors : (i + 1) * vectors] for i in range(4)], axis=0)
    gram = gram_ref[...]
    packed = jnp.concatenate([moments[:half], moments[half:], gram[:half], gram[half:]], axis=1)
    for dest in range(out_ref.shape[0]):
        out_ref[dest] = packed


def final_kernel(recv_ref, sigma_ref, basis_ref, ritz_ref, out_ref):
    total = recv_ref[0]
    for source in range(1, recv_ref.shape[0]):
        total = total + recv_ref[source]
    nb = ritz_ref.shape[0]
    moments = jnp.concatenate([total[:, :nb], total[:, nb : 2 * nb]], axis=0)
    gram = jnp.concatenate([total[:, 2 * nb : 3 * nb], total[:, 3 * nb :]], axis=0)
    ritz = ritz_ref[...]
    dot = functools.partial(jnp.dot, precision=HIGH, preferred_element_type=jnp.float32)
    first = moments - dot(gram, ritz)
    second = first - dot(gram, first)
    weights = ritz + first + second
    out_ref[...] = sigma_ref[...] - lax.dot_general(
        weights, basis_ref[...], TN, precision=HIGH, preferred_element_type=jnp.float32
    )


def shape(*dims, dtype=jnp.float32):
    return jax.ShapeDtypeStruct(dims, dtype)


def call(kernel, outs, ins, operands, scratch=()):
    single = not isinstance(outs, tuple)
    return pl.pallas_call(
        kernel,
        out_shape=outs,
        in_specs=ins,
        out_specs=VMEM if single else (VMEM,) * len(outs),
        scratch_shapes=list(scratch),
        compiler_params=pltpu.CompilerParams(vmem_limit_bytes=16 * 1024 * 1024),
    )(*operands)


def per_device(n_row, n_col, blocks, block_cols, block_slot, trials, basis, ritz_terms):
    local = blocks[0]
    rows, per_row, size, _ = local.shape
    owned = trials[0]
    stored, vectors, _ = owned.shape
    nb, chunk = basis.shape
    cols = jnp.transpose(block_cols, (1, 0, 2))
    half, quarter = nb // 2, nb // 4
    in_hbm = functools.partial(pltpu.with_memory_space_constraint, memory_space=pltpu.HBM)
    quarter = nb // 4
    groups = [list(range(core, n_row, CORES)) for core in range(CORES)]

    packed = call(spread_kernel, shape(n_col, 1, nb * chunk), [VMEM], (basis,))
    packed = lax.all_to_all(packed, "col", 0, 0, tiled=True)
    owned = in_hbm(owned)
    other = lax.ppermute(owned, "row", [(i, i ^ 1) for i in range(n_row)])
    requests = call(
        functools.partial(request_kernel, stored=stored),
        shape(n_row, LANES, dtype=jnp.int32),
        [HBM, HBM],
        (in_hbm(cols), in_hbm(block_slot)),
        [
            pltpu.SMEM(cols.shape, jnp.int32),
            pltpu.SMEM(block_slot.shape, jnp.int32),
            pltpu.SemaphoreType.DMA((2,)),
        ],
    )
    requests, packed, other = lax.optimization_barrier((requests, packed, other))
    wanted = lax.all_to_all(requests, "row", 0, 0, tiled=True, axis_index_groups=groups)
    row_basis = call(
        basis_kernel,
        shape(nb, n_col * chunk),
        [VMEM],
        (packed,),
        [pltpu.VMEM((16, LANES), jnp.float32)],
    )
    gram = call(gram_kernel, shape(nb, nb), [VMEM], (row_basis,))
    sent = call(
        pick_kernel,
        shape(n_row, vectors, size),
        [VMEM, HBM, HBM],
        (wanted, owned, in_hbm(other)),
        [pltpu.VMEM((CORES, stored, vectors, size), jnp.float32), pltpu.SemaphoreType.DMA((2,))],
    )
    sent, local, row_basis, gram = lax.optimization_barrier((sent, local, row_basis, gram))
    chosen = lax.all_to_all(sent, "row", 0, 0, tiled=True, axis_index_groups=groups)

    partial_sums = call(
        functools.partial(partial_kernel, stored),
        shape(n_col, 1, (PACKED + quarter) * LANES),
        [SMEM, SMEM, VMEM, VMEM, VMEM],
        (cols, block_slot, local, chosen, row_basis),
        [pltpu.VMEM((vectors, rows * size), jnp.float32)],
    )
    gathered = lax.all_to_all(partial_sums, "col", 0, 0, tiled=True)
    sigma, keep, moments = call(
        sum_kernel,
        (shape(vectors, chunk), shape(vectors, chunk), shape(n_row, half, LANES)),
        [VMEM, VMEM],
        (gathered, gram),
        [pltpu.VMEM((24, LANES), jnp.float32)],
    )
    all_moments = lax.all_to_all(moments, "row", 0, 0, tiled=True)
    corrections = call(
        final_kernel,
        shape(vectors, chunk),
        [VMEM, VMEM, VMEM, VMEM],
        (all_moments, keep, basis, ritz_terms),
    )
    return sigma, corrections


def solution(mesh):
    in_specs = (
        P("col", "row", None, None, None),
        P("col", "row", None),
        P("col", None),
        P("col", "row", None, None),
        P(None, ("row", "col")),
        P(),
    )
    out_specs = (P(None, ("row", "col")), P(None, ("row", "col")))
    body = functools.partial(per_device, mesh.shape["row"], mesh.shape["col"])
    return jax.shard_map(body, mesh=mesh, in_specs=in_specs, out_specs=out_specs, check_vma=False)
```

```python
import functools

import jax
import jax.numpy as jnp
from jax import lax
from jax.experimental import pallas as pl
from jax.experimental.pallas import tpu as pltpu
from jax.sharding import PartitionSpec as P

LANES = 128
HIGH = lax.Precision.HIGHEST
SMEM = pl.BlockSpec(memory_space=pltpu.SMEM)
VMEM = pl.BlockSpec(memory_space=pltpu.VMEM)
HBM = pl.BlockSpec(memory_space=pltpu.HBM)
NT = (((1,), (1,)), ((), ()))
TN = (((0,), (0,)), ((), ()))
CORES = 2
PACKED = 12
COL_FIRST = 8
ROW_FIRST = 20


def pack(value):
    quarters = [value[8 * i : 8 * i + 8] for i in range(4)]
    cut = LANES - 2 * value.shape[1]
    upper = jnp.concatenate([quarters[0], quarters[1], quarters[2][:, :cut]], axis=1)
    rest = jnp.concatenate([quarters[2][:, cut:], quarters[3]], axis=1)
    return jnp.concatenate([upper, jnp.concatenate([rest[:4], rest[4:]], axis=1)], axis=0)


def unpack(rows, chunk):
    cut = LANES - 2 * chunk
    upper = rows[:8]
    rest = jnp.concatenate([rows[8:, : LANES // 2], rows[8:, LANES // 2 :]], axis=0)
    third = jnp.concatenate([upper[:, 2 * chunk :], rest[:, : chunk - cut]], axis=1)
    return jnp.concatenate(
        [upper[:, :chunk], upper[:, chunk : 2 * chunk], third, rest[:, chunk - cut :]], axis=0
    )


def put_rows(out_ref, group, start, rows):
    for row in range(rows.shape[0]):
        here = slice((start + row) * LANES, (start + row + 1) * LANES)
        out_ref[group, :, here] = rows[row : row + 1]


def slot_of(cols_ref, table_ref, row, entry):
    return table_ref[0, cols_ref[row, 0, entry]]


def spread_kernel(basis_ref, out_ref):
    packed = pack(basis_ref[...])
    for dest in range(out_ref.shape[0]):
        put_rows(out_ref, dest, 0, packed)


def request_kernel(cols_hbm, table_hbm, out_ref, cols, table, sems, *, stored):
    copies = [
        pltpu.make_async_copy(source, target, sems.at[index])
        for index, (source, target) in enumerate([(cols_hbm, cols), (table_hbm, table)])
    ]
    for copy in copies:
        copy.start()
    for copy in copies:
        copy.wait()
    owners = (lax.broadcasted_iota(jnp.int32, out_ref.shape, 0) + ROW_FIRST) % out_ref.shape[0]
    wanted = jnp.zeros(out_ref.shape, jnp.int32)
    for row in range(cols.shape[0]):
        for entry in range(cols.shape[2]):
            slot = slot_of(cols, table, row, entry)
            owner = slot // stored
            wanted = jnp.where(owners == owner, slot - owner * stored, wanted)
    out_ref[...] = wanted


def pick_kernel(wanted_ref, own_hbm, other_hbm, out_ref, pair, sems):
    dests, vectors, size = out_ref.shape
    stored = own_hbm.shape[0]
    core = lax.axis_index("row") % CORES
    copies = [
        pltpu.make_async_copy(own_hbm, pair.at[core], sems.at[0]),
        pltpu.make_async_copy(other_hbm, pair.at[1 - core], sems.at[1]),
    ]
    for copy in copies:
        copy.start()
    for copy in copies:
        copy.wait()
    for dest in range(dests):
        owner = dest % CORES
        want = jnp.broadcast_to(wanted_ref[dest : dest + 1, :], (8, LANES))
        masks = [want == index for index in range(1, stored)]
        for top in range(0, vectors, 8):
            for left in range(0, size, LANES):
                here = (slice(top, top + 8), slice(left, left + LANES))
                tile = pair[owner, 0, *here]
                for index in range(1, stored):
                    tile = jnp.where(masks[index - 1], pair[owner, index, *here], tile)
                out_ref[dest, *here] = tile


def split(value):
    top = value.astype(jnp.bfloat16)
    rest = (value - top.astype(jnp.float32)).astype(jnp.bfloat16)
    return top, rest


def basis_kernel(packed_ref, out_ref, rows):
    groups = packed_ref.shape[0]
    chunk = out_ref.shape[1] // groups
    for group in range(groups):
        place = (group - COL_FIRST) % groups
        for row in range(PACKED):
            rows[row : row + 1] = packed_ref[place, :, row * LANES : (row + 1) * LANES]
        out_ref[:, group * chunk : (group + 1) * chunk] = unpack(rows[:PACKED], chunk)


def gram_kernel(basis_ref, out_ref):
    basis = basis_ref[...]
    out_ref[...] = lax.dot_general(basis, basis, NT, precision=HIGH, preferred_element_type=jnp.float32)


def partial_kernel(stored, cols_ref, table_ref, blocks_ref, chosen_ref, basis_ref, out_ref, part):
    rows, per_row, size, _ = blocks_ref.shape
    vectors = chosen_ref.shape[1]
    groups = out_ref.shape[0]
    for row in range(rows):
        total = jnp.zeros((vectors, size), jnp.float32)
        for entry in range(per_row):
            owner = slot_of(cols_ref, table_ref, row, entry) // stored
            place = (owner + chosen_ref.shape[0] - ROW_FIRST) % chosen_ref.shape[0]
            vec_top, vec_rest = split(chosen_ref[place])
            mat_top, mat_rest = split(blocks_ref[row, entry])
            both = jnp.concatenate([vec_top, vec_rest], axis=0)
            first = lax.dot_general(both, mat_top, NT, preferred_element_type=jnp.float32)
            second = lax.dot_general(vec_top, mat_rest, NT, preferred_element_type=jnp.float32)
            total += first[:vectors] + (first[vectors:] + second)
        part[:, row * size : (row + 1) * size] = total
    moments = lax.dot_general(
        basis_ref[...], part[...], NT, precision=HIGH, preferred_element_type=jnp.float32
    )
    quarter = vectors // 4
    chunk = rows * size // groups
    tail = jnp.concatenate([moments[i * quarter : (i + 1) * quarter] for i in range(4)], axis=1)
    for group in range(groups):
        place = (group - COL_FIRST) % groups
        put_rows(out_ref, place, 0, pack(part[:, group * chunk : (group + 1) * chunk]))
        put_rows(out_ref, place, PACKED, tail)


def sum_kernel(recv_ref, gram_ref, sigma_ref, keep_ref, out_ref, rows):
    vectors, chunk = sigma_ref.shape
    half, quarter = vectors // 2, vectors // 4
    for row in range(PACKED + quarter):
        here = slice(row * LANES, (row + 1) * LANES)
        total = recv_ref[0, :, here]
        for group in range(1, recv_ref.shape[0]):
            total = total + recv_ref[group, :, here]
        place = row if row < PACKED else row - PACKED + 16
        rows[place : place + 1] = total
    sigma = unpack(rows[:PACKED], chunk)
    sigma_ref[...] = sigma
    keep_ref[...] = sigma
    tail = rows[16 : 16 + quarter]
    moments = jnp.concatenate([tail[:, i * vectors : (i + 1) * vectors] for i in range(4)], axis=0)
    gram = gram_ref[...]
    packed = jnp.concatenate([moments[:half], moments[half:], gram[:half], gram[half:]], axis=1)
    for dest in range(out_ref.shape[0]):
        out_ref[dest] = packed


def final_kernel(recv_ref, sigma_ref, basis_ref, ritz_ref, out_ref):
    total = recv_ref[0]
    for source in range(1, recv_ref.shape[0]):
        total = total + recv_ref[source]
    nb = ritz_ref.shape[0]
    moments = jnp.concatenate([total[:, :nb], total[:, nb : 2 * nb]], axis=0)
    gram = jnp.concatenate([total[:, 2 * nb : 3 * nb], total[:, 3 * nb :]], axis=0)
    ritz = ritz_ref[...]
    dot = functools.partial(jnp.dot, precision=HIGH, preferred_element_type=jnp.float32)
    first = moments - dot(gram, ritz)
    second = first - dot(gram, first)
    weights = ritz + first + second
    out_ref[...] = sigma_ref[...] - lax.dot_general(
        weights, basis_ref[...], TN, precision=HIGH, preferred_element_type=jnp.float32
    )


def shape(*dims, dtype=jnp.float32):
    return jax.ShapeDtypeStruct(dims, dtype)


def call(kernel, outs, ins, operands, scratch=()):
    single = not isinstance(outs, tuple)
    return pl.pallas_call(
        kernel,
        out_shape=outs,
        in_specs=ins,
        out_specs=VMEM if single else (VMEM,) * len(outs),
        scratch_shapes=list(scratch),
        compiler_params=pltpu.CompilerParams(vmem_limit_bytes=16 * 1024 * 1024),
    )(*operands)


def turned(count, first):
    return [(first + index) % count for index in range(count)]


def per_device(n_row, n_col, blocks, block_cols, block_slot, trials, basis, ritz_terms):
    local = blocks[0]
    rows, per_row, size, _ = local.shape
    owned = trials[0]
    stored, vectors, _ = owned.shape
    nb, chunk = basis.shape
    cols = jnp.transpose(block_cols, (1, 0, 2))
    half, quarter = nb // 2, nb // 4
    in_hbm = functools.partial(pltpu.with_memory_space_constraint, memory_space=pltpu.HBM)
    quarter = nb // 4
    whole_col = [turned(n_col, COL_FIRST)]
    whole_row = [turned(n_row, ROW_FIRST)]
    groups = [[row for row in whole_row[0] if row % CORES == core] for core in range(CORES)]

    packed = call(spread_kernel, shape(n_col, 1, nb * chunk), [VMEM], (basis,))
    packed = lax.all_to_all(packed, "col", 0, 0, tiled=True, axis_index_groups=whole_col)
    owned = in_hbm(owned)
    other = lax.ppermute(owned, "row", [(i, i ^ 1) for i in range(n_row)])
    requests = call(
        functools.partial(request_kernel, stored=stored),
        shape(n_row, LANES, dtype=jnp.int32),
        [HBM, HBM],
        (in_hbm(cols), in_hbm(block_slot)),
        [
            pltpu.SMEM(cols.shape, jnp.int32),
            pltpu.SMEM(block_slot.shape, jnp.int32),
            pltpu.SemaphoreType.DMA((2,)),
        ],
    )
    requests, packed, other = lax.optimization_barrier((requests, packed, other))
    wanted = lax.all_to_all(requests, "row", 0, 0, tiled=True, axis_index_groups=groups)
    row_basis = call(
        basis_kernel,
        shape(nb, n_col * chunk),
        [VMEM],
        (packed,),
        [pltpu.VMEM((16, LANES), jnp.float32)],
    )
    gram = call(gram_kernel, shape(nb, nb), [VMEM], (row_basis,))
    sent = call(
        pick_kernel,
        shape(n_row, vectors, size),
        [VMEM, HBM, HBM],
        (wanted, owned, in_hbm(other)),
        [pltpu.VMEM((CORES, stored, vectors, size), jnp.float32), pltpu.SemaphoreType.DMA((2,))],
    )
    sent, local, row_basis, gram = lax.optimization_barrier((sent, local, row_basis, gram))
    chosen = lax.all_to_all(sent, "row", 0, 0, tiled=True, axis_index_groups=groups)

    partial_sums = call(
        functools.partial(partial_kernel, stored),
        shape(n_col, 1, (PACKED + quarter) * LANES),
        [SMEM, SMEM, VMEM, VMEM, VMEM],
        (cols, block_slot, local, chosen, row_basis),
        [pltpu.VMEM((vectors, rows * size), jnp.float32)],
    )
    gathered = lax.all_to_all(partial_sums, "col", 0, 0, tiled=True, axis_index_groups=whole_col)
    sigma, keep, moments = call(
        sum_kernel,
        (shape(vectors, chunk), shape(vectors, chunk), shape(n_row, half, LANES)),
        [VMEM, VMEM],
        (gathered, gram),
        [pltpu.VMEM((24, LANES), jnp.float32)],
    )
    all_moments = lax.all_to_all(moments, "row", 0, 0, tiled=True, axis_index_groups=whole_row)
    corrections = call(
        final_kernel,
        shape(vectors, chunk),
        [VMEM, VMEM, VMEM, VMEM],
        (all_moments, keep, basis, ritz_terms),
    )
    return sigma, corrections


def solution(mesh):
    in_specs = (
        P("col", "row", None, None, None),
        P("col", "row", None),
        P("col", None),
        P("col", "row", None, None),
        P(None, ("row", "col")),
        P(),
    )
    out_specs = (P(None, ("row", "col")), P(None, ("row", "col")))
    body = functools.partial(per_device, mesh.shape["row"], mesh.shape["col"])
    return jax.shard_map(body, mesh=mesh, in_specs=in_specs, out_specs=out_specs, check_vma=False)
```

```python
import functools

import jax
import jax.numpy as jnp
from jax import lax
from jax.experimental import pallas as pl
from jax.experimental.pallas import tpu as pltpu
from jax.sharding import PartitionSpec as P

LANES = 128
HIGH = lax.Precision.HIGHEST
SMEM = pl.BlockSpec(memory_space=pltpu.SMEM)
VMEM = pl.BlockSpec(memory_space=pltpu.VMEM)
HBM = pl.BlockSpec(memory_space=pltpu.HBM)
NT = (((1,), (1,)), ((), ()))
TN = (((0,), (0,)), ((), ()))
CORES = 2
PACKED = 12
COL_FIRST = 10
ROW_FIRST = 20


def pack(value):
    quarters = [value[8 * i : 8 * i + 8] for i in range(4)]
    cut = LANES - 2 * value.shape[1]
    upper = jnp.concatenate([quarters[0], quarters[1], quarters[2][:, :cut]], axis=1)
    rest = jnp.concatenate([quarters[2][:, cut:], quarters[3]], axis=1)
    return jnp.concatenate([upper, jnp.concatenate([rest[:4], rest[4:]], axis=1)], axis=0)


def unpack(rows, chunk):
    cut = LANES - 2 * chunk
    upper = rows[:8]
    rest = jnp.concatenate([rows[8:, : LANES // 2], rows[8:, LANES // 2 :]], axis=0)
    third = jnp.concatenate([upper[:, 2 * chunk :], rest[:, : chunk - cut]], axis=1)
    return jnp.concatenate(
        [upper[:, :chunk], upper[:, chunk : 2 * chunk], third, rest[:, chunk - cut :]], axis=0
    )


def put_rows(out_ref, group, start, rows):
    for row in range(rows.shape[0]):
        here = slice((start + row) * LANES, (start + row + 1) * LANES)
        out_ref[group, :, here] = rows[row : row + 1]


def slot_of(cols_ref, table_ref, row, entry):
    return table_ref[0, cols_ref[row, 0, entry]]


def spread_kernel(basis_ref, out_ref):
    packed = pack(basis_ref[...])
    for dest in range(out_ref.shape[0]):
        put_rows(out_ref, dest, 0, packed)


def request_kernel(cols_hbm, table_hbm, out_ref, cols, table, sems, *, stored):
    copies = [
        pltpu.make_async_copy(source, target, sems.at[index])
        for index, (source, target) in enumerate([(cols_hbm, cols), (table_hbm, table)])
    ]
    for copy in copies:
        copy.start()
    for copy in copies:
        copy.wait()
    owners = (lax.broadcasted_iota(jnp.int32, out_ref.shape, 0) + ROW_FIRST) % out_ref.shape[0]
    wanted = jnp.zeros(out_ref.shape, jnp.int32)
    for row in range(cols.shape[0]):
        for entry in range(cols.shape[2]):
            slot = slot_of(cols, table, row, entry)
            owner = slot // stored
            wanted = jnp.where(owners == owner, slot - owner * stored, wanted)
    out_ref[...] = wanted


def pair_kernel(own_hbm, other_hbm, pair, sems):
    core = lax.axis_index("row") % CORES
    copies = [
        pltpu.make_async_copy(own_hbm, pair.at[core], sems.at[0]),
        pltpu.make_async_copy(other_hbm, pair.at[1 - core], sems.at[1]),
    ]
    for copy in copies:
        copy.start()
    for copy in copies:
        copy.wait()


def pick_kernel(wanted_ref, pair, out_ref):
    dests, vectors, size = out_ref.shape
    stored = pair.shape[1]
    for dest in range(dests):
        owner = dest % CORES
        want = jnp.broadcast_to(wanted_ref[dest : dest + 1, :], (8, LANES))
        masks = [want == index for index in range(1, stored)]
        for top in range(0, vectors, 8):
            for left in range(0, size, LANES):
                here = (slice(top, top + 8), slice(left, left + LANES))
                tile = pair[owner, 0, *here]
                for index in range(1, stored):
                    tile = jnp.where(masks[index - 1], pair[owner, index, *here], tile)
                out_ref[dest, *here] = tile


def split(value):
    top = value.astype(jnp.bfloat16)
    rest = (value - top.astype(jnp.float32)).astype(jnp.bfloat16)
    return top, rest


def basis_kernel(packed_ref, out_ref, rows):
    groups = packed_ref.shape[0]
    chunk = out_ref.shape[1] // groups
    for group in range(groups):
        place = (group - COL_FIRST) % groups
        for row in range(PACKED):
            rows[row : row + 1] = packed_ref[place, :, row * LANES : (row + 1) * LANES]
        out_ref[:, group * chunk : (group + 1) * chunk] = unpack(rows[:PACKED], chunk)


def gram_kernel(basis_ref, out_ref):
    basis = basis_ref[...]
    out_ref[...] = lax.dot_general(basis, basis, NT, precision=HIGH, preferred_element_type=jnp.float32)


def partial_kernel(stored, cols_ref, table_ref, blocks_ref, chosen_ref, basis_ref, out_ref, part):
    rows, per_row, size, _ = blocks_ref.shape
    vectors = chosen_ref.shape[1]
    groups = out_ref.shape[0]
    for row in range(rows):
        total = jnp.zeros((vectors, size), jnp.float32)
        for entry in range(per_row):
            owner = slot_of(cols_ref, table_ref, row, entry) // stored
            place = (owner + chosen_ref.shape[0] - ROW_FIRST) % chosen_ref.shape[0]
            vec_top, vec_rest = split(chosen_ref[place])
            mat_top, mat_rest = split(blocks_ref[row, entry])
            both = jnp.concatenate([vec_top, vec_rest], axis=0)
            first = lax.dot_general(both, mat_top, NT, preferred_element_type=jnp.float32)
            second = lax.dot_general(vec_top, mat_rest, NT, preferred_element_type=jnp.float32)
            total += first[:vectors] + (first[vectors:] + second)
        part[:, row * size : (row + 1) * size] = total
    moments = lax.dot_general(
        basis_ref[...], part[...], NT, precision=HIGH, preferred_element_type=jnp.float32
    )
    quarter = vectors // 4
    chunk = rows * size // groups
    tail = jnp.concatenate([moments[i * quarter : (i + 1) * quarter] for i in range(4)], axis=1)
    for group in range(groups):
        place = (group - COL_FIRST) % groups
        put_rows(out_ref, place, 0, pack(part[:, group * chunk : (group + 1) * chunk]))
        put_rows(out_ref, place, PACKED, tail)


def sum_kernel(recv_ref, gram_ref, sigma_ref, keep_ref, out_ref, rows):
    vectors, chunk = sigma_ref.shape
    half, quarter = vectors // 2, vectors // 4
    for row in range(PACKED + quarter):
        here = slice(row * LANES, (row + 1) * LANES)
        total = recv_ref[0, :, here]
        for group in range(1, recv_ref.shape[0]):
            total = total + recv_ref[group, :, here]
        place = row if row < PACKED else row - PACKED + 16
        rows[place : place + 1] = total
    sigma = unpack(rows[:PACKED], chunk)
    sigma_ref[...] = sigma
    keep_ref[...] = sigma
    tail = rows[16 : 16 + quarter]
    moments = jnp.concatenate([tail[:, i * vectors : (i + 1) * vectors] for i in range(4)], axis=0)
    gram = gram_ref[...]
    packed = jnp.concatenate([moments[:half], moments[half:], gram[:half], gram[half:]], axis=1)
    for dest in range(out_ref.shape[0]):
        out_ref[dest] = packed


def final_kernel(recv_ref, sigma_ref, basis_ref, ritz_ref, out_ref):
    total = recv_ref[0]
    for source in range(1, recv_ref.shape[0]):
        total = total + recv_ref[source]
    nb = ritz_ref.shape[0]
    moments = jnp.concatenate([total[:, :nb], total[:, nb : 2 * nb]], axis=0)
    gram = jnp.concatenate([total[:, 2 * nb : 3 * nb], total[:, 3 * nb :]], axis=0)
    ritz = ritz_ref[...]
    dot = functools.partial(jnp.dot, precision=HIGH, preferred_element_type=jnp.float32)
    turn = functools.partial(
        lax.dot_general, dimension_numbers=TN, precision=HIGH, preferred_element_type=jnp.float32
    )
    basis = basis_ref[...]
    first = moments - dot(gram, ritz)
    both = 2.0 * basis - turn(gram, basis)
    out_ref[...] = (sigma_ref[...] - turn(ritz, basis)) - turn(first, both)


def shape(*dims, dtype=jnp.float32):
    return jax.ShapeDtypeStruct(dims, dtype)


def call(kernel, outs, ins, operands, scratch=()):
    single = not isinstance(outs, tuple)
    return pl.pallas_call(
        kernel,
        out_shape=outs,
        in_specs=ins,
        out_specs=VMEM if single else (VMEM,) * len(outs),
        scratch_shapes=list(scratch),
        compiler_params=pltpu.CompilerParams(vmem_limit_bytes=16 * 1024 * 1024),
    )(*operands)


def turned(count, first):
    return [(first + index) % count for index in range(count)]


def per_device(n_row, n_col, blocks, block_cols, block_slot, trials, basis, ritz_terms):
    local = blocks[0]
    rows, per_row, size, _ = local.shape
    owned = trials[0]
    stored, vectors, _ = owned.shape
    nb, chunk = basis.shape
    cols = jnp.transpose(block_cols, (1, 0, 2))
    half, quarter = nb // 2, nb // 4
    in_hbm = functools.partial(pltpu.with_memory_space_constraint, memory_space=pltpu.HBM)
    quarter = nb // 4
    whole_col = [turned(n_col, COL_FIRST)]
    whole_row = [turned(n_row, ROW_FIRST)]
    groups = [[row for row in whole_row[0] if row % CORES == core] for core in range(CORES)]

    packed = call(spread_kernel, shape(n_col, 1, nb * chunk), [VMEM], (basis,))
    packed = lax.all_to_all(packed, "col", 0, 0, tiled=True, axis_index_groups=whole_col)
    owned = in_hbm(owned)
    other = lax.ppermute(owned, "row", [(i, i ^ 1) for i in range(n_row)])
    requests = call(
        functools.partial(request_kernel, stored=stored),
        shape(n_row, LANES, dtype=jnp.int32),
        [HBM, HBM],
        (in_hbm(cols), in_hbm(block_slot)),
        [
            pltpu.SMEM(cols.shape, jnp.int32),
            pltpu.SMEM(block_slot.shape, jnp.int32),
            pltpu.SemaphoreType.DMA((2,)),
        ],
    )
    requests, packed, other = lax.optimization_barrier((requests, packed, other))
    wanted = lax.all_to_all(requests, "row", 0, 0, tiled=True, axis_index_groups=groups)
    row_basis = call(
        basis_kernel,
        shape(nb, n_col * chunk),
        [VMEM],
        (packed,),
        [pltpu.VMEM((16, LANES), jnp.float32)],
    )
    gram = call(gram_kernel, shape(nb, nb), [VMEM], (row_basis,))
    pair = call(
        pair_kernel,
        shape(CORES, stored, vectors, size),
        [HBM, HBM],
        (owned, in_hbm(other)),
        [pltpu.SemaphoreType.DMA((2,))],
    )
    sent = call(pick_kernel, shape(n_row, vectors, size), [VMEM, VMEM], (wanted, pair))
    sent, local, row_basis, gram = lax.optimization_barrier((sent, local, row_basis, gram))
    chosen = lax.all_to_all(sent, "row", 0, 0, tiled=True, axis_index_groups=groups)

    partial_sums = call(
        functools.partial(partial_kernel, stored),
        shape(n_col, 1, (PACKED + quarter) * LANES),
        [SMEM, SMEM, VMEM, VMEM, VMEM],
        (cols, block_slot, local, chosen, row_basis),
        [pltpu.VMEM((vectors, rows * size), jnp.float32)],
    )
    gathered = lax.all_to_all(partial_sums, "col", 0, 0, tiled=True, axis_index_groups=whole_col)
    sigma, keep, moments = call(
        sum_kernel,
        (shape(vectors, chunk), shape(vectors, chunk), shape(n_row, half, LANES)),
        [VMEM, VMEM],
        (gathered, gram),
        [pltpu.VMEM((24, LANES), jnp.float32)],
    )
    all_moments = lax.all_to_all(moments, "row", 0, 0, tiled=True, axis_index_groups=whole_row)
    corrections = call(
        final_kernel,
        shape(vectors, chunk),
        [VMEM, VMEM, VMEM, VMEM],
        (all_moments, keep, basis, ritz_terms),
    )
    return sigma, corrections


def solution(mesh):
    in_specs = (
        P("col", "row", None, None, None),
        P("col", "row", None),
        P("col", None),
        P("col", "row", None, None),
        P(None, ("row", "col")),
        P(),
    )
    out_specs = (P(None, ("row", "col")), P(None, ("row", "col")))
    body = functools.partial(per_device, mesh.shape["row"], mesh.shape["col"])
    return jax.shard_map(body, mesh=mesh, in_specs=in_specs, out_specs=out_specs, check_vma=False)
```

```python
import functools

import jax
import jax.numpy as jnp
from jax import lax
from jax.experimental import pallas as pl
from jax.experimental.pallas import tpu as pltpu
from jax.sharding import PartitionSpec as P

LANES = 128
HIGH = lax.Precision.HIGHEST
SMEM = pl.BlockSpec(memory_space=pltpu.SMEM)
VMEM = pl.BlockSpec(memory_space=pltpu.VMEM)
HBM = pl.BlockSpec(memory_space=pltpu.HBM)
NT = (((1,), (1,)), ((), ()))
TN = (((0,), (0,)), ((), ()))
CORES = 2
PACKED = 12
COL_FIRST = 10
ROW_FIRST = 20


def pack(value):
    quarters = [value[8 * i : 8 * i + 8] for i in range(4)]
    cut = LANES - 2 * value.shape[1]
    upper = jnp.concatenate([quarters[0], quarters[1], quarters[2][:, :cut]], axis=1)
    rest = jnp.concatenate([quarters[2][:, cut:], quarters[3]], axis=1)
    return jnp.concatenate([upper, jnp.concatenate([rest[:4], rest[4:]], axis=1)], axis=0)


def unpack(rows, chunk):
    cut = LANES - 2 * chunk
    upper = rows[:8]
    rest = jnp.concatenate([rows[8:, : LANES // 2], rows[8:, LANES // 2 :]], axis=0)
    third = jnp.concatenate([upper[:, 2 * chunk :], rest[:, : chunk - cut]], axis=1)
    return jnp.concatenate(
        [upper[:, :chunk], upper[:, chunk : 2 * chunk], third, rest[:, chunk - cut :]], axis=0
    )


def put_rows(out_ref, group, start, rows):
    for row in range(rows.shape[0]):
        here = slice((start + row) * LANES, (start + row + 1) * LANES)
        out_ref[group, :, here] = rows[row : row + 1]


def slot_of(cols_ref, table_ref, row, entry):
    return table_ref[0, cols_ref[row, 0, entry]]


def spread_kernel(basis_ref, out_ref):
    packed = pack(basis_ref[...])
    for dest in range(out_ref.shape[0]):
        put_rows(out_ref, dest, 0, packed)


def request_kernel(cols_hbm, table_hbm, out_ref, cols, table, sems, *, stored):
    copies = [
        pltpu.make_async_copy(source, target, sems.at[index])
        for index, (source, target) in enumerate([(cols_hbm, cols), (table_hbm, table)])
    ]
    for copy in copies:
        copy.start()
    for copy in copies:
        copy.wait()
    owners = (lax.broadcasted_iota(jnp.int32, out_ref.shape, 0) + ROW_FIRST) % out_ref.shape[0]
    wanted = jnp.zeros(out_ref.shape, jnp.int32)
    for row in range(cols.shape[0]):
        for entry in range(cols.shape[2]):
            slot = slot_of(cols, table, row, entry)
            owner = slot // stored
            wanted = jnp.where(owners == owner, slot - owner * stored, wanted)
    out_ref[...] = wanted


def pair_kernel(own_hbm, other_hbm, pair, sems):
    core = lax.axis_index("row") % CORES
    copies = [
        pltpu.make_async_copy(own_hbm, pair.at[core], sems.at[0]),
        pltpu.make_async_copy(other_hbm, pair.at[1 - core], sems.at[1]),
    ]
    for copy in copies:
        copy.start()
    for copy in copies:
        copy.wait()


def pick_kernel(wanted_ref, pair, out_ref):
    dests, vectors, size = out_ref.shape
    stored = pair.shape[1]
    for dest in range(dests):
        owner = dest % CORES
        want = jnp.broadcast_to(wanted_ref[dest : dest + 1, :], (8, LANES))
        masks = [want == index for index in range(1, stored)]
        for top in range(0, vectors, 8):
            for left in range(0, size, LANES):
                here = (slice(top, top + 8), slice(left, left + LANES))
                tile = pair[owner, 0, *here]
                for index in range(1, stored):
                    tile = jnp.where(masks[index - 1], pair[owner, index, *here], tile)
                out_ref[dest, *here] = tile


def split(value):
    top = value.astype(jnp.bfloat16)
    rest = (value - top.astype(jnp.float32)).astype(jnp.bfloat16)
    return top, rest


def fold(value):
    quarter = value.shape[0] // 4
    return jnp.concatenate([value[i * quarter : (i + 1) * quarter] for i in range(4)], axis=1)


def unfold(rows):
    width = rows.shape[1] // 4
    return jnp.concatenate([rows[:, i * width : (i + 1) * width] for i in range(4)], axis=0)


def basis_kernel(packed_ref, out_ref, gram_ref, rows):
    groups = packed_ref.shape[0]
    chunk = out_ref.shape[1] // groups
    for group in range(groups):
        place = (group - COL_FIRST) % groups
        for row in range(PACKED):
            rows[row : row + 1] = packed_ref[place, :, row * LANES : (row + 1) * LANES]
        out_ref[:, group * chunk : (group + 1) * chunk] = unpack(rows[:PACKED], chunk)
    basis = out_ref[...]
    gram_ref[...] = fold(
        lax.dot_general(basis, basis, NT, precision=HIGH, preferred_element_type=jnp.float32)
    )


def partial_kernel(stored, cols_ref, table_ref, blocks_ref, chosen_ref, basis_ref, out_ref, part):
    rows, per_row, size, _ = blocks_ref.shape
    vectors = chosen_ref.shape[1]
    groups = out_ref.shape[0]
    for row in range(rows):
        total = jnp.zeros((vectors, size), jnp.float32)
        for entry in range(per_row):
            owner = slot_of(cols_ref, table_ref, row, entry) // stored
            place = (owner + chosen_ref.shape[0] - ROW_FIRST) % chosen_ref.shape[0]
            vec_top, vec_rest = split(chosen_ref[place])
            mat_top, mat_rest = split(blocks_ref[row, entry])
            both = jnp.concatenate([vec_top, vec_rest], axis=0)
            first = lax.dot_general(both, mat_top, NT, preferred_element_type=jnp.float32)
            second = lax.dot_general(vec_top, mat_rest, NT, preferred_element_type=jnp.float32)
            total += first[:vectors] + (first[vectors:] + second)
        part[:, row * size : (row + 1) * size] = total
    moments = lax.dot_general(
        basis_ref[...], part[...], NT, precision=HIGH, preferred_element_type=jnp.float32
    )
    quarter = vectors // 4
    chunk = rows * size // groups
    tail = jnp.concatenate([moments[i * quarter : (i + 1) * quarter] for i in range(4)], axis=1)
    for group in range(groups):
        place = (group - COL_FIRST) % groups
        put_rows(out_ref, place, 0, pack(part[:, group * chunk : (group + 1) * chunk]))
        put_rows(out_ref, place, PACKED, tail)


def sum_kernel(recv_ref, gram_ref, sigma_ref, out_ref, rows):
    vectors, chunk = sigma_ref.shape
    quarter = vectors // 4
    for row in range(PACKED + quarter):
        here = slice(row * LANES, (row + 1) * LANES)
        total = recv_ref[0, :, here]
        for group in range(1, recv_ref.shape[0]):
            total = total + recv_ref[group, :, here]
        place = row if row < PACKED else row - PACKED + 16
        rows[place : place + 1] = total
    packed = jnp.concatenate([rows[16 : 16 + quarter], gram_ref[...]], axis=0)
    for dest in range(out_ref.shape[0]):
        out_ref[dest] = packed
    sigma_ref[...] = unpack(rows[:PACKED], chunk)


def final_kernel(recv_ref, kept_ref, basis_ref, ritz_ref, sigma_ref, out_ref):
    total = recv_ref[0]
    for source in range(1, recv_ref.shape[0]):
        total = total + recv_ref[source]
    quarter = total.shape[0] // 2
    moments, gram = unfold(total[:quarter]), unfold(total[quarter:])
    ritz, basis, sigma = ritz_ref[...], basis_ref[...], kept_ref[...]
    dot = functools.partial(jnp.dot, precision=HIGH, preferred_element_type=jnp.float32)
    turn = functools.partial(
        lax.dot_general, dimension_numbers=TN, precision=HIGH, preferred_element_type=jnp.float32
    )
    sigma_ref[...] = sigma
    first = moments - dot(gram, ritz)
    both = 2.0 * basis - turn(gram, basis)
    out_ref[...] = (sigma - turn(ritz, basis)) - turn(first, both)


def shape(*dims, dtype=jnp.float32):
    return jax.ShapeDtypeStruct(dims, dtype)


def call(kernel, outs, ins, operands, scratch=()):
    single = not isinstance(outs, tuple)
    return pl.pallas_call(
        kernel,
        out_shape=outs,
        in_specs=ins,
        out_specs=VMEM if single else (VMEM,) * len(outs),
        scratch_shapes=list(scratch),
        compiler_params=pltpu.CompilerParams(vmem_limit_bytes=16 * 1024 * 1024),
    )(*operands)


def turned(count, first):
    return [(first + index) % count for index in range(count)]


def per_device(n_row, n_col, blocks, block_cols, block_slot, trials, basis, ritz_terms):
    local = blocks[0]
    rows, per_row, size, _ = local.shape
    owned = trials[0]
    stored, vectors, _ = owned.shape
    nb, chunk = basis.shape
    cols = jnp.transpose(block_cols, (1, 0, 2))
    quarter = nb // 4
    in_hbm = functools.partial(pltpu.with_memory_space_constraint, memory_space=pltpu.HBM)
    quarter = nb // 4
    whole_col = [turned(n_col, COL_FIRST)]
    whole_row = [turned(n_row, ROW_FIRST)]
    groups = [[row for row in whole_row[0] if row % CORES == core] for core in range(CORES)]

    packed = call(spread_kernel, shape(n_col, 1, nb * chunk), [VMEM], (basis,))
    packed = lax.all_to_all(packed, "col", 0, 0, tiled=True, axis_index_groups=whole_col)
    owned = in_hbm(owned)
    other = lax.ppermute(owned, "row", [(i, i ^ 1) for i in range(n_row)])
    requests = call(
        functools.partial(request_kernel, stored=stored),
        shape(n_row, LANES, dtype=jnp.int32),
        [HBM, HBM],
        (in_hbm(cols), in_hbm(block_slot)),
        [
            pltpu.SMEM(cols.shape, jnp.int32),
            pltpu.SMEM(block_slot.shape, jnp.int32),
            pltpu.SemaphoreType.DMA((2,)),
        ],
    )
    requests, packed, other = lax.optimization_barrier((requests, packed, other))
    wanted = lax.all_to_all(requests, "row", 0, 0, tiled=True, axis_index_groups=groups)
    row_basis, gram = call(
        basis_kernel,
        (shape(nb, n_col * chunk), shape(quarter, LANES)),
        [VMEM],
        (packed,),
        [pltpu.VMEM((16, LANES), jnp.float32)],
    )
    pair = call(
        pair_kernel,
        shape(CORES, stored, vectors, size),
        [HBM, HBM],
        (owned, in_hbm(other)),
        [pltpu.SemaphoreType.DMA((2,))],
    )
    sent = call(pick_kernel, shape(n_row, vectors, size), [VMEM, VMEM], (wanted, pair))
    sent, local, row_basis, gram = lax.optimization_barrier((sent, local, row_basis, gram))
    chosen = lax.all_to_all(sent, "row", 0, 0, tiled=True, axis_index_groups=groups)

    partial_sums = call(
        functools.partial(partial_kernel, stored),
        shape(n_col, 1, (PACKED + quarter) * LANES),
        [SMEM, SMEM, VMEM, VMEM, VMEM],
        (cols, block_slot, local, chosen, row_basis),
        [pltpu.VMEM((vectors, rows * size), jnp.float32)],
    )
    gathered = lax.all_to_all(partial_sums, "col", 0, 0, tiled=True, axis_index_groups=whole_col)
    kept, moments = call(
        sum_kernel,
        (shape(vectors, chunk), shape(n_row, 2 * quarter, LANES)),
        [VMEM, VMEM],
        (gathered, gram),
        [pltpu.VMEM((24, LANES), jnp.float32)],
    )
    all_moments = lax.all_to_all(moments, "row", 0, 0, tiled=True, axis_index_groups=whole_row)
    sigma, corrections = call(
        final_kernel,
        (shape(vectors, chunk), shape(vectors, chunk)),
        [VMEM, VMEM, VMEM, VMEM],
        (all_moments, kept, basis, ritz_terms),
    )
    return sigma, corrections


def solution(mesh):
    in_specs = (
        P("col", "row", None, None, None),
        P("col", "row", None),
        P("col", None),
        P("col", "row", None, None),
        P(None, ("row", "col")),
        P(),
    )
    out_specs = (P(None, ("row", "col")), P(None, ("row", "col")))
    body = functools.partial(per_device, mesh.shape["row"], mesh.shape["col"])
    return jax.shard_map(body, mesh=mesh, in_specs=in_specs, out_specs=out_specs, check_vma=False)
```

```python
import functools

import jax
import jax.numpy as jnp
from jax import lax
from jax.experimental import pallas as pl
from jax.experimental.pallas import tpu as pltpu
from jax.sharding import PartitionSpec as P

LANES = 128
HIGH = lax.Precision.HIGHEST
SMEM = pl.BlockSpec(memory_space=pltpu.SMEM)
VMEM = pl.BlockSpec(memory_space=pltpu.VMEM)
HBM = pl.BlockSpec(memory_space=pltpu.HBM)
NT = (((1,), (1,)), ((), ()))
TN = (((0,), (0,)), ((), ()))
CORES = 2
PACKED = 12
COL_FIRST = 10
ROW_FIRST = 20


def pack(value):
    quarters = [value[8 * i : 8 * i + 8] for i in range(4)]
    cut = LANES - 2 * value.shape[1]
    upper = jnp.concatenate([quarters[0], quarters[1], quarters[2][:, :cut]], axis=1)
    rest = jnp.concatenate([quarters[2][:, cut:], quarters[3]], axis=1)
    return jnp.concatenate([upper, jnp.concatenate([rest[:4], rest[4:]], axis=1)], axis=0)


def unpack(rows, chunk):
    cut = LANES - 2 * chunk
    upper = rows[:8]
    rest = jnp.concatenate([rows[8:, : LANES // 2], rows[8:, LANES // 2 :]], axis=0)
    third = jnp.concatenate([upper[:, 2 * chunk :], rest[:, : chunk - cut]], axis=1)
    return jnp.concatenate(
        [upper[:, :chunk], upper[:, chunk : 2 * chunk], third, rest[:, chunk - cut :]], axis=0
    )


def put_rows(out_ref, group, start, rows):
    for row in range(rows.shape[0]):
        here = slice((start + row) * LANES, (start + row + 1) * LANES)
        out_ref[group, :, here] = rows[row : row + 1]


def slot_of(cols_ref, table_ref, row, entry):
    return table_ref[0, cols_ref[row, 0, entry]]


def spread_kernel(basis_ref, out_ref):
    packed = pack(basis_ref[...])
    for dest in range(out_ref.shape[0]):
        put_rows(out_ref, dest, 0, packed)


def request_kernel(cols_hbm, table_hbm, out_ref, cols, table, sems, *, stored):
    copies = [
        pltpu.make_async_copy(source, target, sems.at[index])
        for index, (source, target) in enumerate([(cols_hbm, cols), (table_hbm, table)])
    ]
    for copy in copies:
        copy.start()
    for copy in copies:
        copy.wait()
    owners = (lax.broadcasted_iota(jnp.int32, out_ref.shape, 0) + ROW_FIRST) % out_ref.shape[0]
    wanted = jnp.zeros(out_ref.shape, jnp.int32)
    for row in range(cols.shape[0]):
        for entry in range(cols.shape[2]):
            slot = slot_of(cols, table, row, entry)
            owner = slot // stored
            wanted = jnp.where(owners == owner, slot - owner * stored, wanted)
    out_ref[...] = wanted


def pair_kernel(own_hbm, other_hbm, pair, sems):
    core = lax.axis_index("row") % CORES
    copies = [
        pltpu.make_async_copy(own_hbm, pair.at[core], sems.at[0]),
        pltpu.make_async_copy(other_hbm, pair.at[1 - core], sems.at[1]),
    ]
    for copy in copies:
        copy.start()
    for copy in copies:
        copy.wait()


def pick_kernel(wanted_ref, pair, out_ref):
    dests, vectors, size = out_ref.shape
    stored = pair.shape[1]
    for dest in range(dests):
        owner = dest % CORES
        want = jnp.broadcast_to(wanted_ref[dest : dest + 1, :], (8, LANES))
        masks = [want == index for index in range(1, stored)]
        for top in range(0, vectors, 8):
            for left in range(0, size, LANES):
                here = (slice(top, top + 8), slice(left, left + LANES))
                tile = pair[owner, 0, *here]
                for index in range(1, stored):
                    tile = jnp.where(masks[index - 1], pair[owner, index, *here], tile)
                out_ref[dest, *here] = tile


def split(value):
    top = value.astype(jnp.bfloat16)
    rest = (value - top.astype(jnp.float32)).astype(jnp.bfloat16)
    return top, rest


def fold(value):
    quarter = value.shape[0] // 4
    return jnp.concatenate([value[i * quarter : (i + 1) * quarter] for i in range(4)], axis=1)


def unfold(rows):
    width = rows.shape[1] // 4
    return jnp.concatenate([rows[:, i * width : (i + 1) * width] for i in range(4)], axis=0)


def basis_kernel(packed_ref, out_ref, gram_ref, rows):
    groups = packed_ref.shape[0]
    chunk = out_ref.shape[1] // groups
    for group in range(groups):
        place = (group - COL_FIRST) % groups
        for row in range(PACKED):
            rows[row : row + 1] = packed_ref[place, :, row * LANES : (row + 1) * LANES]
        out_ref[:, group * chunk : (group + 1) * chunk] = unpack(rows[:PACKED], chunk)
    basis = out_ref[...]
    gram_ref[...] = fold(
        lax.dot_general(basis, basis, NT, precision=HIGH, preferred_element_type=jnp.float32)
    )


def partial_kernel(
    stored,
    cols_hbm,
    table_hbm,
    blocks_ref,
    chosen_ref,
    basis_ref,
    out_ref,
    part,
    cols_ref,
    table_ref,
    tops,
    rests,
    sems,
):
    rows, per_row, size, _ = blocks_ref.shape
    vectors = chosen_ref.shape[1]
    groups = out_ref.shape[0]
    copies = [
        pltpu.make_async_copy(cols_hbm, cols_ref, sems.at[0]),
        pltpu.make_async_copy(table_hbm, table_ref, sems.at[1]),
    ]
    for copy in copies:
        copy.start()
    for entry in range(per_row):
        tops[entry], rests[entry] = split(blocks_ref[0, entry])
    for copy in copies:
        copy.wait()
    for row in range(rows):
        total = jnp.zeros((vectors, size), jnp.float32)
        for entry in range(per_row):
            owner = slot_of(cols_ref, table_ref, row, entry) // stored
            place = (owner + chosen_ref.shape[0] - ROW_FIRST) % chosen_ref.shape[0]
            vec_top, vec_rest = split(chosen_ref[place])
            if row == 0:
                mat_top, mat_rest = tops[entry], rests[entry]
            else:
                mat_top, mat_rest = split(blocks_ref[row, entry])
            both = jnp.concatenate([vec_top, vec_rest], axis=0)
            first = lax.dot_general(both, mat_top, NT, preferred_element_type=jnp.float32)
            second = lax.dot_general(vec_top, mat_rest, NT, preferred_element_type=jnp.float32)
            total += first[:vectors] + (first[vectors:] + second)
        part[:, row * size : (row + 1) * size] = total
    moments = lax.dot_general(
        basis_ref[...], part[...], NT, precision=HIGH, preferred_element_type=jnp.float32
    )
    quarter = vectors // 4
    chunk = rows * size // groups
    tail = jnp.concatenate([moments[i * quarter : (i + 1) * quarter] for i in range(4)], axis=1)
    for group in range(groups):
        place = (group - COL_FIRST) % groups
        put_rows(out_ref, place, 0, pack(part[:, group * chunk : (group + 1) * chunk]))
        put_rows(out_ref, place, PACKED, tail)


def sum_kernel(recv_ref, gram_ref, sigma_ref, out_ref, rows):
    vectors, chunk = sigma_ref.shape
    quarter = vectors // 4
    for row in range(PACKED + quarter):
        here = slice(row * LANES, (row + 1) * LANES)
        total = recv_ref[0, :, here]
        for group in range(1, recv_ref.shape[0]):
            total = total + recv_ref[group, :, here]
        place = row if row < PACKED else row - PACKED + 16
        rows[place : place + 1] = total
    packed = jnp.concatenate([rows[16 : 16 + quarter], gram_ref[...]], axis=0)
    for dest in range(out_ref.shape[0]):
        out_ref[dest] = packed
    sigma_ref[...] = unpack(rows[:PACKED], chunk)


def final_kernel(recv_ref, kept_ref, basis_ref, ritz_ref, sigma_ref, out_ref):
    total = recv_ref[0]
    for source in range(1, recv_ref.shape[0]):
        total = total + recv_ref[source]
    quarter = total.shape[0] // 2
    moments, gram = unfold(total[:quarter]), unfold(total[quarter:])
    ritz, basis, sigma = ritz_ref[...], basis_ref[...], kept_ref[...]
    dot = functools.partial(jnp.dot, precision=HIGH, preferred_element_type=jnp.float32)
    turn = functools.partial(
        lax.dot_general, dimension_numbers=TN, precision=HIGH, preferred_element_type=jnp.float32
    )
    sigma_ref[...] = sigma
    first = moments - dot(gram, ritz)
    both = 2.0 * basis - turn(gram, basis)
    out_ref[...] = (sigma - turn(ritz, basis)) - turn(first, both)


def shape(*dims, dtype=jnp.float32):
    return jax.ShapeDtypeStruct(dims, dtype)


def call(kernel, outs, ins, operands, scratch=()):
    single = not isinstance(outs, tuple)
    return pl.pallas_call(
        kernel,
        out_shape=outs,
        in_specs=ins,
        out_specs=VMEM if single else (VMEM,) * len(outs),
        scratch_shapes=list(scratch),
        compiler_params=pltpu.CompilerParams(vmem_limit_bytes=16 * 1024 * 1024),
    )(*operands)


def turned(count, first):
    return [(first + index) % count for index in range(count)]


def per_device(n_row, n_col, blocks, block_cols, block_slot, trials, basis, ritz_terms):
    local = blocks[0]
    rows, per_row, size, _ = local.shape
    owned = trials[0]
    stored, vectors, _ = owned.shape
    nb, chunk = basis.shape
    cols = jnp.transpose(block_cols, (1, 0, 2))
    quarter = nb // 4
    in_hbm = functools.partial(pltpu.with_memory_space_constraint, memory_space=pltpu.HBM)
    quarter = nb // 4
    whole_col = [turned(n_col, COL_FIRST)]
    whole_row = [turned(n_row, ROW_FIRST)]
    groups = [[row for row in whole_row[0] if row % CORES == core] for core in range(CORES)]

    packed = call(spread_kernel, shape(n_col, 1, nb * chunk), [VMEM], (basis,))
    packed = lax.all_to_all(packed, "col", 0, 0, tiled=True, axis_index_groups=whole_col)
    owned = in_hbm(owned)
    other = lax.ppermute(owned, "row", [(i, i ^ 1) for i in range(n_row)])
    requests = call(
        functools.partial(request_kernel, stored=stored),
        shape(n_row, LANES, dtype=jnp.int32),
        [HBM, HBM],
        (in_hbm(cols), in_hbm(block_slot)),
        [
            pltpu.SMEM(cols.shape, jnp.int32),
            pltpu.SMEM(block_slot.shape, jnp.int32),
            pltpu.SemaphoreType.DMA((2,)),
        ],
    )
    requests, packed, other = lax.optimization_barrier((requests, packed, other))
    wanted = lax.all_to_all(requests, "row", 0, 0, tiled=True, axis_index_groups=groups)
    row_basis, gram = call(
        basis_kernel,
        (shape(nb, n_col * chunk), shape(quarter, LANES)),
        [VMEM],
        (packed,),
        [pltpu.VMEM((16, LANES), jnp.float32)],
    )
    pair = call(
        pair_kernel,
        shape(CORES, stored, vectors, size),
        [HBM, HBM],
        (owned, in_hbm(other)),
        [pltpu.SemaphoreType.DMA((2,))],
    )
    sent = call(pick_kernel, shape(n_row, vectors, size), [VMEM, VMEM], (wanted, pair))
    sent, local, row_basis, gram = lax.optimization_barrier((sent, local, row_basis, gram))
    chosen = lax.all_to_all(sent, "row", 0, 0, tiled=True, axis_index_groups=groups)

    partial_sums = call(
        functools.partial(partial_kernel, stored),
        shape(n_col, 1, (PACKED + quarter) * LANES),
        [HBM, HBM, VMEM, VMEM, VMEM],
        (in_hbm(cols), in_hbm(block_slot), local, chosen, row_basis),
        [
            pltpu.VMEM((vectors, rows * size), jnp.float32),
            pltpu.SMEM(cols.shape, jnp.int32),
            pltpu.SMEM(block_slot.shape, jnp.int32),
            pltpu.VMEM((per_row, size, size), jnp.bfloat16),
            pltpu.VMEM((per_row, size, size), jnp.bfloat16),
            pltpu.SemaphoreType.DMA((2,)),
        ],
    )
    gathered = lax.all_to_all(partial_sums, "col", 0, 0, tiled=True, axis_index_groups=whole_col)
    kept, moments = call(
        sum_kernel,
        (shape(vectors, chunk), shape(n_row, 2 * quarter, LANES)),
        [VMEM, VMEM],
        (gathered, gram),
        [pltpu.VMEM((24, LANES), jnp.float32)],
    )
    all_moments = lax.all_to_all(moments, "row", 0, 0, tiled=True, axis_index_groups=whole_row)
    sigma, corrections = call(
        final_kernel,
        (shape(vectors, chunk), shape(vectors, chunk)),
        [VMEM, VMEM, VMEM, VMEM],
        (all_moments, kept, basis, ritz_terms),
    )
    return sigma, corrections


def solution(mesh):
    in_specs = (
        P("col", "row", None, None, None),
        P("col", "row", None),
        P("col", None),
        P("col", "row", None, None),
        P(None, ("row", "col")),
        P(),
    )
    out_specs = (P(None, ("row", "col")), P(None, ("row", "col")))
    body = functools.partial(per_device, mesh.shape["row"], mesh.shape["col"])
    return jax.shard_map(body, mesh=mesh, in_specs=in_specs, out_specs=out_specs, check_vma=False)
```

```python
import functools

import jax
import jax.numpy as jnp
from jax import lax
from jax.experimental import pallas as pl
from jax.experimental.pallas import tpu as pltpu
from jax.sharding import PartitionSpec as P

LANES = 128
HIGH = lax.Precision.HIGHEST
SMEM = pl.BlockSpec(memory_space=pltpu.SMEM)
VMEM = pl.BlockSpec(memory_space=pltpu.VMEM)
HBM = pl.BlockSpec(memory_space=pltpu.HBM)
NT = (((1,), (1,)), ((), ()))
TN = (((0,), (0,)), ((), ()))
CORES = 2
PACKED = 12
COL_FIRST = 9
ROW_FIRST = 20


def pack(value):
    quarters = [value[8 * i : 8 * i + 8] for i in range(4)]
    cut = LANES - 2 * value.shape[1]
    upper = jnp.concatenate([quarters[0], quarters[1], quarters[2][:, :cut]], axis=1)
    rest = jnp.concatenate([quarters[2][:, cut:], quarters[3]], axis=1)
    return jnp.concatenate([upper, jnp.concatenate([rest[:4], rest[4:]], axis=1)], axis=0)


def unpack(rows, chunk):
    cut = LANES - 2 * chunk
    upper = rows[:8]
    rest = jnp.concatenate([rows[8:, : LANES // 2], rows[8:, LANES // 2 :]], axis=0)
    third = jnp.concatenate([upper[:, 2 * chunk :], rest[:, : chunk - cut]], axis=1)
    return jnp.concatenate(
        [upper[:, :chunk], upper[:, chunk : 2 * chunk], third, rest[:, chunk - cut :]], axis=0
    )


def put_rows(out_ref, group, start, rows):
    for row in range(rows.shape[0]):
        here = slice((start + row) * LANES, (start + row + 1) * LANES)
        out_ref[group, :, here] = rows[row : row + 1]


def slot_of(cols_ref, table_ref, row, entry):
    return table_ref[0, cols_ref[row, 0, entry]]


def spread_kernel(basis_ref, out_ref):
    packed = pack(basis_ref[...])
    for dest in range(out_ref.shape[0]):
        put_rows(out_ref, dest, 0, packed)


def request_kernel(cols_hbm, table_hbm, out_ref, cols, table, sems, *, stored):
    copies = [
        pltpu.make_async_copy(source, target, sems.at[index])
        for index, (source, target) in enumerate([(cols_hbm, cols), (table_hbm, table)])
    ]
    for copy in copies:
        copy.start()
    for copy in copies:
        copy.wait()
    owners = (lax.broadcasted_iota(jnp.int32, out_ref.shape, 0) + ROW_FIRST) % out_ref.shape[0]
    wanted = jnp.zeros(out_ref.shape, jnp.int32)
    for row in range(cols.shape[0]):
        for entry in range(cols.shape[2]):
            slot = slot_of(cols, table, row, entry)
            owner = slot // stored
            wanted = jnp.where(owners == owner, slot - owner * stored, wanted)
    out_ref[...] = wanted


def pair_kernel(own_hbm, other_hbm, pair, sems):
    core = lax.axis_index("row") % CORES
    copies = [
        pltpu.make_async_copy(own_hbm, pair.at[core], sems.at[0]),
        pltpu.make_async_copy(other_hbm, pair.at[1 - core], sems.at[1]),
    ]
    for copy in copies:
        copy.start()
    for copy in copies:
        copy.wait()


def pick_kernel(wanted_ref, pair, out_ref):
    dests, vectors, size = out_ref.shape
    stored = pair.shape[1]
    for dest in range(dests):
        owner = dest % CORES
        want = jnp.broadcast_to(wanted_ref[dest : dest + 1, :], (8, LANES))
        masks = [want == index for index in range(1, stored)]
        for top in range(0, vectors, 8):
            for left in range(0, size, LANES):
                here = (slice(top, top + 8), slice(left, left + LANES))
                tile = pair[owner, 0, *here]
                for index in range(1, stored):
                    tile = jnp.where(masks[index - 1], pair[owner, index, *here], tile)
                out_ref[dest, *here] = tile


def split(value):
    top = value.astype(jnp.bfloat16)
    rest = (value - top.astype(jnp.float32)).astype(jnp.bfloat16)
    return top, rest


def fold(value):
    quarter = value.shape[0] // 4
    return jnp.concatenate([value[i * quarter : (i + 1) * quarter] for i in range(4)], axis=1)


def unfold(rows):
    width = rows.shape[1] // 4
    return jnp.concatenate([rows[:, i * width : (i + 1) * width] for i in range(4)], axis=0)


def basis_kernel(packed_ref, out_ref, gram_ref, rows):
    groups = packed_ref.shape[0]
    chunk = out_ref.shape[1] // groups
    for group in range(groups):
        place = (group - COL_FIRST) % groups
        for row in range(PACKED):
            rows[row : row + 1] = packed_ref[place, :, row * LANES : (row + 1) * LANES]
        out_ref[:, group * chunk : (group + 1) * chunk] = unpack(rows[:PACKED], chunk)
    basis = out_ref[...]
    gram_ref[...] = fold(
        lax.dot_general(basis, basis, NT, precision=HIGH, preferred_element_type=jnp.float32)
    )


def partial_kernel(stored, cols_ref, table_ref, blocks_ref, chosen_ref, basis_ref, out_ref, part):
    rows, per_row, size, _ = blocks_ref.shape
    vectors = chosen_ref.shape[1]
    groups = out_ref.shape[0]
    for row in range(rows):
        total = jnp.zeros((vectors, size), jnp.float32)
        for entry in range(per_row):
            owner = slot_of(cols_ref, table_ref, row, entry) // stored
            place = (owner + chosen_ref.shape[0] - ROW_FIRST) % chosen_ref.shape[0]
            vec_top, vec_rest = split(chosen_ref[place])
            mat_top, mat_rest = split(blocks_ref[row, entry])
            both = jnp.concatenate([vec_top, vec_rest], axis=0)
            first = lax.dot_general(both, mat_top, NT, preferred_element_type=jnp.float32)
            second = lax.dot_general(vec_top, mat_rest, NT, preferred_element_type=jnp.float32)
            total += first[:vectors] + (first[vectors:] + second)
        part[:, row * size : (row + 1) * size] = total
    moments = lax.dot_general(
        basis_ref[...], part[...], NT, precision=HIGH, preferred_element_type=jnp.float32
    )
    quarter = vectors // 4
    chunk = rows * size // groups
    tail = jnp.concatenate([moments[i * quarter : (i + 1) * quarter] for i in range(4)], axis=1)
    for group in range(groups):
        place = (group - COL_FIRST) % groups
        put_rows(out_ref, place, 0, pack(part[:, group * chunk : (group + 1) * chunk]))
        put_rows(out_ref, place, PACKED, tail)


def sum_kernel(recv_ref, gram_ref, sigma_ref, out_ref, rows):
    vectors, chunk = sigma_ref.shape
    quarter = vectors // 4
    for row in range(PACKED + quarter):
        here = slice(row * LANES, (row + 1) * LANES)
        total = recv_ref[0, :, here]
        for group in range(1, recv_ref.shape[0]):
            total = total + recv_ref[group, :, here]
        place = row if row < PACKED else row - PACKED + 16
        rows[place : place + 1] = total
    packed = jnp.concatenate([rows[16 : 16 + quarter], gram_ref[...]], axis=0)
    for dest in range(out_ref.shape[0]):
        out_ref[dest] = packed
    sigma_ref[...] = unpack(rows[:PACKED], chunk)


def final_kernel(recv_ref, kept_ref, basis_ref, ritz_ref, sigma_ref, out_ref):
    total = recv_ref[0]
    for source in range(1, recv_ref.shape[0]):
        total = total + recv_ref[source]
    quarter = total.shape[0] // 2
    moments, gram = unfold(total[:quarter]), unfold(total[quarter:])
    ritz, basis, sigma = ritz_ref[...], basis_ref[...], kept_ref[...]
    dot = functools.partial(jnp.dot, precision=HIGH, preferred_element_type=jnp.float32)
    turn = functools.partial(
        lax.dot_general, dimension_numbers=TN, precision=HIGH, preferred_element_type=jnp.float32
    )
    sigma_ref[...] = sigma
    first = moments - dot(gram, ritz)
    both = 2.0 * basis - turn(gram, basis)
    out_ref[...] = (sigma - turn(ritz, basis)) - turn(first, both)


def shape(*dims, dtype=jnp.float32):
    return jax.ShapeDtypeStruct(dims, dtype)


def call(kernel, outs, ins, operands, scratch=()):
    single = not isinstance(outs, tuple)
    return pl.pallas_call(
        kernel,
        out_shape=outs,
        in_specs=ins,
        out_specs=VMEM if single else (VMEM,) * len(outs),
        scratch_shapes=list(scratch),
        compiler_params=pltpu.CompilerParams(vmem_limit_bytes=16 * 1024 * 1024),
    )(*operands)


def turned(count, first):
    return [(first + index) % count for index in range(count)]


def per_device(n_row, n_col, blocks, block_cols, block_slot, trials, basis, ritz_terms):
    local = blocks[0]
    rows, per_row, size, _ = local.shape
    owned = trials[0]
    stored, vectors, _ = owned.shape
    nb, chunk = basis.shape
    cols = jnp.transpose(block_cols, (1, 0, 2))
    quarter = nb // 4
    in_hbm = functools.partial(pltpu.with_memory_space_constraint, memory_space=pltpu.HBM)
    quarter = nb // 4
    whole_col = [turned(n_col, COL_FIRST)]
    whole_row = [turned(n_row, ROW_FIRST)]
    groups = [[row for row in whole_row[0] if row % CORES == core] for core in range(CORES)]

    packed = call(spread_kernel, shape(n_col, 1, nb * chunk), [VMEM], (basis,))
    packed = lax.all_to_all(packed, "col", 0, 0, tiled=True, axis_index_groups=whole_col)
    owned = in_hbm(owned)
    other = lax.ppermute(owned, "row", [(i, i ^ 1) for i in range(n_row)])
    requests = call(
        functools.partial(request_kernel, stored=stored),
        shape(n_row, LANES, dtype=jnp.int32),
        [HBM, HBM],
        (in_hbm(cols), in_hbm(block_slot)),
        [
            pltpu.SMEM(cols.shape, jnp.int32),
            pltpu.SMEM(block_slot.shape, jnp.int32),
            pltpu.SemaphoreType.DMA((2,)),
        ],
    )
    requests, packed, other = lax.optimization_barrier((requests, packed, other))
    wanted = lax.all_to_all(requests, "row", 0, 0, tiled=True, axis_index_groups=groups)
    row_basis, gram = call(
        basis_kernel,
        (shape(nb, n_col * chunk), shape(quarter, LANES)),
        [VMEM],
        (packed,),
        [pltpu.VMEM((16, LANES), jnp.float32)],
    )
    pair = call(
        pair_kernel,
        shape(CORES, stored, vectors, size),
        [HBM, HBM],
        (owned, in_hbm(other)),
        [pltpu.SemaphoreType.DMA((2,))],
    )
    sent = call(pick_kernel, shape(n_row, vectors, size), [VMEM, VMEM], (wanted, pair))
    sent, local, row_basis, gram = lax.optimization_barrier((sent, local, row_basis, gram))
    chosen = lax.all_to_all(sent, "row", 0, 0, tiled=True, axis_index_groups=groups)

    partial_sums = call(
        functools.partial(partial_kernel, stored),
        shape(n_col, 1, (PACKED + quarter) * LANES),
        [SMEM, SMEM, VMEM, VMEM, VMEM],
        (cols, block_slot, local, chosen, row_basis),
        [pltpu.VMEM((vectors, rows * size), jnp.float32)],
    )
    gathered = lax.all_to_all(partial_sums, "col", 0, 0, tiled=True, axis_index_groups=whole_col)
    kept, moments = call(
        sum_kernel,
        (shape(vectors, chunk), shape(n_row, 2 * quarter, LANES)),
        [VMEM, VMEM],
        (gathered, gram),
        [pltpu.VMEM((24, LANES), jnp.float32)],
    )
    all_moments = lax.all_to_all(moments, "row", 0, 0, tiled=True, axis_index_groups=whole_row)
    sigma, corrections = call(
        final_kernel,
        (shape(vectors, chunk), shape(vectors, chunk)),
        [VMEM, VMEM, VMEM, VMEM],
        (all_moments, kept, basis, ritz_terms),
    )
    return sigma, corrections


def solution(mesh):
    in_specs = (
        P("col", "row", None, None, None),
        P("col", "row", None),
        P("col", None),
        P("col", "row", None, None),
        P(None, ("row", "col")),
        P(),
    )
    out_specs = (P(None, ("row", "col")), P(None, ("row", "col")))
    body = functools.partial(per_device, mesh.shape["row"], mesh.shape["col"])
    return jax.shard_map(body, mesh=mesh, in_specs=in_specs, out_specs=out_specs, check_vma=False)
```
